32 devices in a mesh: groups: 2 (over x), tm: 8 (over z, y), rows: 2 (over core).
Axes of the slice: x: 2, y: 2, z: 4, core: 2. Of those that a mesh axis runs over, the one named last changes fastest.
Arguments:
- frames_in: bfloat16 [4, 8, 16, 256, 128], P('groups', 'tm', 'rows'), parts along dimension 0, may hold values from -12 to 12
- gain_one: float32 [128], replicated, may hold values from 0.25 to 1.75
- norm_bias_one: float32 [128], replicated, may hold values from -3 to 3
- kernel_one: bfloat16 [3, 3, 3, 128, 128], replicated, may hold values from -0.109375 to 0.109375
- bias_one: float32 [128], replicated, may hold values from -2 to 2
- gain_two: float32 [128], replicated, may hold values from 0.25 to 1.75
- norm_bias_two: float32 [128], replicated, may hold values from -3 to 3
- kernel_two: bfloat16 [3, 3, 3, 128, 128], replicated, may hold values from -0.109375 to 0.109375
- bias_two: float32 [128], replicated, may hold values from -2 to 2
- kernel_down: bfloat16 [3, 3, 128, 128], replicated, may hold values from -0.1875 to 0.1875
- bias_down: float32 [128], replicated, may hold values from -2 to 2
Outputs:
- features_down: bfloat16 [4, 8, 8, 128, 128], P('groups', 'tm', 'rows'), parts along dimension 0
The draws below stay inside these ranges and needn't reach their ends.
There are 2 independent parts, one for each index of `groups`. The reference program is written for one: setup_inputs(seed, part) draws one part's arguments, and reference() takes and returns one part's arrays. A program takes and returns all parts, laid end to end along the dimension named above; an argument that names none is the same for every part. Nothing has to cross between parts.
All inputs are finite; a program needn't handle non-finite values.
Results may differ from the reference program's by a relative error of at most 0.0095.
Values may be sent and summed in bfloat16 or wider, within the bound.
A program may use at most 128 MiB of HBM per device.

```python
import jax
import jax.numpy as jnp
from jax import lax

C = 128
G = 32
CLIPS = 2
W = 256
FRAMES = 8
H = 16


def draw_frames_in(key, part):
    key_base = jax.random.fold_in(key, 11)
    key_frame = jax.random.fold_in(key, 12)
    key_offset = jax.random.fold_in(key, 13)
    shape = (CLIPS, FRAMES, H, W, C)
    positions = jnp.arange(H, dtype=jnp.float32) / (H - 1)
    frame_scale = jax.random.uniform(key_frame, (CLIPS, FRAMES, 1, 1, 1), minval=0.5, maxval=1.5)
    offset = 0.3 * jax.random.normal(key_offset, (CLIPS, FRAMES, 1, 1, C))
    base = jax.random.normal(key_base, shape)
    row_scale = 0.6 * jnp.exp(jnp.log(3.0) * positions)
    values = base * frame_scale * row_scale[None, None, :, None, None] + offset
    return jnp.clip(values, -12.0, 12.0).astype(jnp.bfloat16)


def bell_draw(stream_key, dims, scale, most, kind=jnp.bfloat16):
    drawn = jax.random.normal(stream_key, dims, jnp.float32) * scale
    return jnp.minimum(jnp.maximum(drawn, -most), most).astype(kind)


def setup_inputs(seed: int = 0, part: int = 0) -> dict:
    seeds = jax.random.split(jax.random.key(seed), 12)
    own_keys = jax.random.split(jax.random.fold_in(seeds[11], part), 12)
    frames_in = draw_frames_in(jax.random.fold_in(jax.random.fold_in(seeds[11], part), 71), part)
    gain_one = jnp.clip(1.0 + 0.15 * jax.random.normal(seeds[1], (C,), jnp.float32), 0.25, 1.75)
    norm_bias_one = bell_draw(seeds[2], (C,), 0.5, 3.0, jnp.float32)
    kernel_one = bell_draw(seeds[3], (3, 3, 3, C, C), (27 * C) ** -0.5, 0.109375)
    bias_one = bell_draw(seeds[4], (C,), 0.3, 2.0, jnp.float32)
    gain_two = jnp.clip(1.0 + 0.15 * jax.random.normal(seeds[5], (C,), jnp.float32), 0.25, 1.75)
    norm_bias_two = bell_draw(seeds[6], (C,), 0.5, 3.0, jnp.float32)
    kernel_two = bell_draw(seeds[7], (3, 3, 3, C, C), (27 * C) ** -0.5, 0.109375)
    bias_two = bell_draw(seeds[8], (C,), 0.3, 2.0, jnp.float32)
    kernel_down = bell_draw(seeds[9], (3, 3, C, C), (9 * C) ** -0.5, 0.1875)
    bias_down = bell_draw(seeds[10], (C,), 0.3, 2.0, jnp.float32)
    return {"frames_in": frames_in, "gain_one": gain_one, "norm_bias_one": norm_bias_one, "kernel_one": kernel_one, "bias_one": bias_one, "gain_two": gain_two, "norm_bias_two": norm_bias_two, "kernel_two": kernel_two, "bias_two": bias_two, "kernel_down": kernel_down, "bias_down": bias_down}


EPSILON = 1e-06

def normalize(values, gain, bias):
    batch, frames, height, width, channels = values.shape
    grouped = values.reshape(batch, frames, height, width, G, channels // G)
    average = lax.optimization_barrier(jnp.mean(grouped, axis=(2, 3, 5), keepdims=True))
    mean_square = lax.optimization_barrier(jnp.mean(grouped * grouped, axis=(2, 3, 5), keepdims=True))
    inverse = lax.rsqrt(mean_square - average * average + EPSILON)
    scaled = ((grouped - average) * inverse).reshape(values.shape) * gain + bias
    return jax.nn.silu(scaled).astype(jnp.bfloat16)

def causal_conv(normed, kernel, bias):
    batch, frames, height, width, channels = normed.shape
    values = normed.astype(jnp.float32)
    padded = jnp.concatenate([values[:, :1], values[:, :1], values], axis=1)
    stacked = jnp.concatenate([padded[:, 0:frames], padded[:, 1:frames + 1], padded[:, 2:frames + 2]], axis=-1)
    stacked = stacked.reshape(batch * frames, height, width, 3 * channels)
    weights = kernel.astype(jnp.float32).reshape(3, 3, 3 * channels, channels)
    result = lax.conv_general_dilated(stacked, weights, (1, 1), ((1, 1), (1, 1)), dimension_numbers=('NHWC', 'HWIO', 'NHWC'), precision=lax.Precision.HIGHEST, preferred_element_type=jnp.float32)
    return result.reshape(batch, frames, height, width, channels) + bias

def reference(frames_in, gain_one, norm_bias_one, kernel_one, bias_one, gain_two, norm_bias_two, kernel_two, bias_two, kernel_down, bias_down):
    batch, frames, height, width, channels = frames_in.shape
    inputs = frames_in.astype(jnp.float32)
    hidden_one = causal_conv(normalize(inputs, gain_one, norm_bias_one), kernel_one, bias_one).astype(jnp.bfloat16)
    normed_two = normalize(hidden_one.astype(jnp.float32), gain_two, norm_bias_two)
    residual = (inputs + causal_conv(normed_two, kernel_two, bias_two)).astype(jnp.bfloat16)
    flat = residual.astype(jnp.float32).reshape(batch * frames, height, width, channels)
    padded = jnp.pad(flat, ((0, 0), (0, 1), (0, 1), (0, 0)))
    result = lax.conv_general_dilated(padded, kernel_down.astype(jnp.float32), (2, 2), 'VALID', dimension_numbers=('NHWC', 'HWIO', 'NHWC'), precision=lax.Precision.HIGHEST, preferred_element_type=jnp.float32)
    result = result + bias_down
    return result.reshape(batch, frames, height // 2, width // 2, channels).astype(jnp.bfloat16)
```

```python
import jax
import jax.numpy as jnp
from jax import lax
from jax.experimental import pallas as pl
from jax.experimental.pallas import tpu as pltpu
from jax.sharding import PartitionSpec as P

G = 32


EPSILON = 1e-06

MESH = pl.DeviceIdType.MESH


def build(batch, height, width, channels, steps, bands):
    half = height // 2
    quarter = width // 2
    C = channels

    def kernel(
        x_ref, scales_ref, k1_ref, k2_ref, kd_ref, out_ref,
        field, weights, down, hidden, paired, spread, sums, others,
        k_sem, own2_sem, own1_sem, relay_sem, in2_sem, in1_sem,
        edge_out, edge_in, sums_out, sums_in, res_out, res_in,
    ):
        t = lax.axis_index("tm")
        r = lax.axis_index("rows")
        has1 = t >= 1
        has2 = t >= 2
        odd = lax.rem(t, 2) == 1
        sends2 = t + 2 < steps
        sends1 = jnp.logical_and(
            t + 1 < steps, jnp.logical_or(jnp.logical_not(odd), t + 2 >= steps)
        )
        relays = jnp.logical_and(odd, has2)
        slots = [jnp.maximum(f, 2 - t) for f in range(3)]
        present = [has2, has1, None]

        loads = []
        for cv, k_ref in enumerate((k1_ref, k2_ref)):
            for a in range(3):
                for b in range(3):
                    for o in range(2):
                        loads.append(
                            (
                                k_ref.at[a, b],
                                weights.at[
                                    cv,
                                    pl.ds((a + o) * 3 * C, 3 * C),
                                    pl.ds((o * 3 + b) * C, C),
                                ],
                            )
                        )
        conv_loads = len(loads) // 2
        for a in range(3):
            for b in range(3):
                loads.append(
                    (
                        kd_ref.at[a, b],
                        down.at[
                            pl.ds(a * 2 * C + (C if b == 1 else 0), C),
                            pl.ds(C if b == 2 else 0, C),
                        ],
                    )
                )
        loads = [
            pltpu.make_async_copy(src, dst, k_sem.at[n])
            for n, (src, dst) in enumerate(loads)
        ]
        for load in loads:
            load.start()

        barrier = pltpu.get_barrier_semaphore()
        expected = bands - 1
        for off in range(1, bands):
            pl.semaphore_signal(
                barrier, inc=1, device_id={"rows": lax.rem(r + off, bands)}, device_id_type=MESH
            )
        for by in (-2, -1, 1, 2):
            there = jnp.logical_and(t + by >= 0, t + by < steps)
            expected = expected + there.astype(jnp.int32)

            @pl.when(there)
            def _():
                pl.semaphore_signal(
                    barrier, inc=1, device_id={"tm": t + by}, device_id_type=MESH
                )

        zero_block = jnp.zeros((3 * C, C), jnp.bfloat16)
        for cv in range(2):
            for b in range(3):
                weights[cv, 9 * C : 12 * C, b * C : (b + 1) * C] = zero_block
                weights[cv, 0 : 3 * C, (3 + b) * C : (4 + b) * C] = zero_block
        for a in range(3):
            down[(2 * a + 1) * C : (2 * a + 2) * C, C : 2 * C] = jnp.zeros((C, C), jnp.bfloat16)

        @pl.when(r == 0)
        def _():
            for cv in range(2):
                for clip in range(batch):
                    for f in range(3):
                        field[cv, clip, f, 0] = jnp.zeros((width, C), jnp.bfloat16)

        @pl.when(r == bands - 1)
        def _():
            for cv in range(2):
                for clip in range(batch):
                    for f in range(3):
                        field[cv, clip, f, height + 1] = jnp.zeros((width, C), jnp.bfloat16)
            for clip in range(batch):
                paired[clip, height] = jnp.zeros((quarter, 2 * C), jnp.bfloat16)

        def rows_of(cv, clip, slot, q):
            return field.at[cv, clip, slot, pl.ds(1 + 2 * q, 2)]

        def own2(cv, clip, q):
            return pltpu.make_async_remote_copy(
                src_ref=rows_of(cv, clip, 2, q), dst_ref=rows_of(cv, clip, 0, q),
                send_sem=own2_sem.at[cv, clip, q], recv_sem=in2_sem.at[cv, clip, q],
                device_id={"tm": t + 2}, device_id_type=MESH,
            )

        def own1(cv, clip, q):
            return pltpu.make_async_remote_copy(
                src_ref=rows_of(cv, clip, 2, q), dst_ref=rows_of(cv, clip, 1, q),
                send_sem=own1_sem.at[cv, clip, q], recv_sem=in1_sem.at[cv, clip, q],
                device_id={"tm": t + 1}, device_id_type=MESH,
            )

        def relay(cv, clip, q):
            return pltpu.make_async_remote_copy(
                src_ref=rows_of(cv, clip, 0, q), dst_ref=rows_of(cv, clip, 1, q),
                send_sem=relay_sem.at[cv, clip, q], recv_sem=in1_sem.at[cv, clip, q],
                device_id={"tm": t - 1}, device_id_type=MESH,
            )

        def edge(cv, clip, slot, way):
            src, dst, by = ((1, height + 1, -1), (height, 0, 1))[way]
            return pltpu.make_async_remote_copy(
                src_ref=field.at[cv, clip, slot, src], dst_ref=field.at[cv, clip, slot, dst],
                send_sem=edge_out.at[cv, clip, slot, way],
                recv_sem=edge_in.at[cv, clip, slot, way],
                device_id={"rows": r + by}, device_id_type=MESH,
            )

        def totals(cv, clip, off):
            return pltpu.make_async_remote_copy(
                src_ref=sums.at[cv, clip], dst_ref=others.at[cv, clip, off - 1],
                send_sem=sums_out.at[cv, clip, off - 1], recv_sem=sums_in.at[cv, clip, off - 1],
                device_id={"rows": lax.rem(r + off, bands)}, device_id_type=MESH,
            )

        def below(clip):
            return pltpu.make_async_remote_copy(
                src_ref=paired.at[clip, 0], dst_ref=paired.at[clip, height],
                send_sem=res_out.at[clip], recv_sem=res_in.at[clip],
                device_id={"rows": r - 1}, device_id_type=MESH,
            )

        def when(condition, action):
            if condition is None:
                action()
            else:
                pl.when(condition)(action)

        def both(first, second):
            return second if first is None else jnp.logical_and(first, second)

        upper = r > 0
        lower = r < bands - 1

        def start_edges(cv, clip, slot):
            when(both(present[slot], upper), lambda: edge(cv, clip, slot, 0).start())
            when(both(present[slot], lower), lambda: edge(cv, clip, slot, 1).start())

        def wait_edges(cv, clip, slot):
            when(both(present[slot], lower), lambda: edge(cv, clip, slot, 0).wait_recv())
            when(both(present[slot], upper), lambda: edge(cv, clip, slot, 1).wait_recv())

        def folded(values):
            return jnp.sum(values.reshape(width // 8, 8, C), axis=0)

        def start_totals(cv, clip, total, square):
            sums[cv, clip, 0:8] = total
            sums[cv, clip, 8:16] = square
            for off in range(1, bands):
                totals(cv, clip, off).start()

        lane = lax.broadcasted_iota(jnp.int32, (1, C), 1)
        size = C // G

        def grouped(values):
            result = values
            for k in range(1, size):
                left = pltpu.roll(values, k, 1)
                right = pltpu.roll(values, C - k, 1)
                result = result + jnp.where(lax.rem(lane, size) >= k, left, 0.0)
                result = result + jnp.where(lax.rem(lane, size) < size - k, right, 0.0)
            return result

        def constants(cv, clip):
            total = sums[cv, clip]
            for off in range(1, bands):
                totals(cv, clip, off).wait_recv()
                total = total + others[cv, clip, off - 1]
            entries = height * bands * width * size
            sum1 = jnp.broadcast_to(jnp.sum(total[0:8], axis=0, keepdims=True), (8, C))
            sum2 = jnp.broadcast_to(jnp.sum(total[8:16], axis=0, keepdims=True), (8, C))
            average = grouped(sum1)[0:1] / entries
            mean_square = grouped(sum2)[0:1] / entries
            inverse = lax.rsqrt(mean_square - average * average + EPSILON)
            return average, inverse * scales_ref[3 * cv : 3 * cv + 1], scales_ref[3 * cv + 1 : 3 * cv + 2]

        def normalize(cv, clip, source):
            average, scale, shift = constants(cv, clip)

            def step(q, _):
                for i in range(2):
                    v = source[clip, 2 * q + i].astype(jnp.float32)
                    s = 0.5 * ((v - average) * scale + shift)
                    field[cv, clip, 2, 1 + 2 * q + i] = (s + s * jnp.tanh(s)).astype(jnp.bfloat16)
                when(sends2, lambda: own2(cv, clip, q).start())
                when(sends1, lambda: own1(cv, clip, q).start())
                return 0

            lax.fori_loop(0, half, step, 0)
            start_edges(cv, clip, 2)

        def receive(cv, clip):
            def second(q, _):
                own2(cv, clip, q).wait_recv()
                when(relays, lambda: relay(cv, clip, q).start())
                return 0

            def first(q, _):
                own1(cv, clip, q).wait_recv()
                return 0

            @pl.when(has2)
            def _():
                lax.fori_loop(0, half, second, 0)

            start_edges(cv, clip, 0)

            @pl.when(has1)
            def _():
                lax.fori_loop(0, half, first, 0)

            start_edges(cv, clip, 1)
            for slot in (2, 0, 1):
                wait_edges(cv, clip, slot)

        column = lax.broadcasted_iota(jnp.int32, (width, 1), 0)

        def convolved(cv, clip, p):
            x = jnp.concatenate(
                [field[cv, clip, slots[f], 2 * p + d] for d in range(4) for f in range(3)], axis=1
            )
            dot = lambda a, b: jnp.dot(a, b, preferred_element_type=jnp.float32)
            y0 = dot(x[:, : 9 * C], weights[cv, : 9 * C, : 2 * C])
            y1 = dot(x, weights[cv, :, 2 * C : 4 * C])
            y2 = dot(x[:, 3 * C :], weights[cv, 3 * C :, 4 * C :])
            bias = scales_ref[3 * cv + 2 : 3 * cv + 3]

            def joined(left, middle, right):
                left = jnp.where(column >= 1, pltpu.roll(left, 1, 0), 0.0)
                right = jnp.where(column < width - 1, pltpu.roll(right, width - 1, 0), 0.0)
                return middle + left + right + bias

            return (
                joined(y0[:, :C], y0[:, C:], y1[:, :C]),
                joined(y1[:, C:], y2[:, :C], y2[:, C:]),
            )

        def conv_one(clip):
            def step(p, carry):
                total, square = carry
                for i, y in enumerate(convolved(0, clip, p)):
                    y = y.astype(jnp.bfloat16)
                    hidden[clip, 2 * p + i] = y
                    y = y.astype(jnp.float32)
                    total = total + folded(y)
                    square = square + folded(y * y)
                return total, square

            zero = jnp.zeros((8, C), jnp.float32)
            start_totals(0 + 1, clip, *lax.fori_loop(0, half, step, (zero, zero)))

        def conv_two(clip):
            def step(p, _):
                for i, y in enumerate(convolved(1, clip, p)):
                    y = y + x_ref[clip, 2 * p + i].astype(jnp.float32)
                    spread[i] = y.astype(jnp.bfloat16).astype(jnp.float32)
                    even = spread[i, pl.ds(0, quarter, stride=2), :]
                    uneven = spread[i, pl.ds(1, quarter, stride=2), :]
                    paired[clip, 2 * p + i] = jnp.concatenate(
                        [even.astype(jnp.bfloat16), uneven.astype(jnp.bfloat16)], axis=1
                    )
                return 0

            step(0, 0)
            when(upper, lambda: below(clip).start())
            lax.fori_loop(1, half, step, 0)

        narrow = lax.broadcasted_iota(jnp.int32, (quarter, 1), 0)

        def downsample(clip):
            when(lower, lambda: below(clip).wait_recv())
            for i in range(half):
                x = jnp.concatenate([paired[clip, 2 * i + a] for a in range(3)], axis=1)
                y = jnp.dot(x, down[...], preferred_element_type=jnp.float32)
                right = pltpu.roll(y[:, C:], quarter - 1, 0)
                y = y[:, :C] + jnp.where(narrow < quarter - 1, right, 0.0) + scales_ref[6:7]
                out_ref[clip, i] = y.astype(jnp.bfloat16)

        for clip in range(batch):
            def gather(i, carry):
                v = x_ref[clip, i].astype(jnp.float32)
                return carry[0] + folded(v), carry[1] + folded(v * v)

            zero = jnp.zeros((8, C), jnp.float32)
            found = lax.fori_loop(0, height, gather, (zero, zero))
            if clip == 0:
                pl.semaphore_wait(barrier, expected)
            start_totals(0, clip, *found)
        for clip in range(batch):
            normalize(0, clip, x_ref)
        for load in loads[:conv_loads]:
            load.wait()
        for clip in range(batch):
            receive(0, clip)
            conv_one(clip)
            normalize(1, clip, hidden)
        for load in loads[conv_loads:]:
            load.wait()
        for clip in range(batch):
            receive(1, clip)
            conv_two(clip)
            downsample(clip)

        for cv in range(2):
            for clip in range(batch):
                def leave(q, _):
                    when(sends2, lambda: own2(cv, clip, q).wait_send())
                    when(sends1, lambda: own1(cv, clip, q).wait_send())
                    when(relays, lambda: relay(cv, clip, q).wait_send())
                    return 0

                lax.fori_loop(0, half, leave, 0)
                for slot in range(3):
                    when(both(present[slot], upper), lambda: edge(cv, clip, slot, 0).wait_send())
                    when(both(present[slot], lower), lambda: edge(cv, clip, slot, 1).wait_send())
                for off in range(1, bands):
                    totals(cv, clip, off).wait_send()
        for clip in range(batch):
            when(upper, lambda: below(clip).wait_send())

    vmem = pl.BlockSpec(memory_space=pltpu.VMEM)
    hbm = pl.BlockSpec(memory_space=pl.ANY)
    dma = pltpu.SemaphoreType.DMA
    return pl.pallas_call(
        kernel,
        out_shape=jax.ShapeDtypeStruct((batch, half, quarter, C), jnp.bfloat16),
        in_specs=[vmem, vmem, hbm, hbm, hbm],
        out_specs=vmem,
        scratch_shapes=[
            pltpu.VMEM((2, batch, 3, height + 2, width, C), jnp.bfloat16),
            pltpu.VMEM((2, 12 * C, 6 * C), jnp.bfloat16),
            pltpu.VMEM((6 * C, 2 * C), jnp.bfloat16),
            pltpu.VMEM((batch, height, width, C), jnp.bfloat16),
            pltpu.VMEM((batch, height + 1, quarter, 2 * C), jnp.bfloat16),
            pltpu.VMEM((2, width, C), jnp.float32),
            pltpu.VMEM((2, batch, 16, C), jnp.float32),
            pltpu.VMEM((2, batch, max(bands - 1, 1), 16, C), jnp.float32),
            dma((45,)),
            dma((2, batch, half)),
            dma((2, batch, half)),
            dma((2, batch, half)),
            dma((2, batch, half)),
            dma((2, batch, half)),
            dma((2, batch, 3, 2)),
            dma((2, batch, 3, 2)),
            dma((2, batch, max(bands - 1, 1))),
            dma((2, batch, max(bands - 1, 1))),
            dma((batch,)),
            dma((batch,)),
        ],
        compiler_params=pltpu.CompilerParams(
            collective_id=0, has_side_effects=True, vmem_limit_bytes=50 * 1024 * 1024
        ),
    )


def solution(mesh):
    steps, bands = mesh.shape["tm"], mesh.shape["rows"]

    def local(
        frames_in,
        gain_one,
        norm_bias_one,
        kernel_one,
        bias_one,
        gain_two,
        norm_bias_two,
        kernel_two,
        bias_two,
        kernel_down,
        bias_down,
    ):
        inputs = frames_in[:, 0]
        batch, height, width, channels = inputs.shape
        scales = jnp.stack(
            [gain_one, norm_bias_one, bias_one, gain_two, norm_bias_two, bias_two, bias_down, bias_down]
        )
        wide = (3, 3, 3 * channels, channels)
        call = build(batch, height, width, channels, steps, bands)
        result = call(
            inputs, scales, kernel_one.reshape(wide), kernel_two.reshape(wide), kernel_down
        )
        return result[:, None]

    placed = (P("groups", "tm", "rows", None, None),) + (P(),) * 10
    return jax.shard_map(
        local,
        mesh=mesh,
        in_specs=placed,
        out_specs=P("groups", "tm", "rows", None, None),
        check_vma=False,
    )
```

```python
import jax
import jax.numpy as jnp
from jax import lax
from jax.experimental import pallas as pl
from jax.experimental.pallas import tpu as pltpu
from jax.sharding import PartitionSpec as P

G = 32


EPSILON = 1e-06

MESH = pl.DeviceIdType.MESH


def build(batch, height, width, channels, steps, bands):
    half = height // 2
    quarter = width // 2
    C = channels

    def kernel(
        frames_ref, g1_ref, n1_ref, c1_ref, g2_ref, n2_ref, c2_ref, cd_ref,
        k1_ref, k2_ref, kd_ref, out_ref,
        x_ref, scales, field, weights, down, hidden, paired, spread, sums, others,
        x_sem, scale_sem, k_sem, own2_sem, own1_sem, relay_sem, in2_sem, in1_sem,
        edge_out, edge_in, sums_out, sums_in, res_out, res_in,
    ):
        t = lax.axis_index("tm")
        r = lax.axis_index("rows")
        has1 = t >= 1
        has2 = t >= 2
        odd = lax.rem(t, 2) == 1
        sends2 = t + 2 < steps
        sends1 = jnp.logical_and(
            t + 1 < steps, jnp.logical_or(jnp.logical_not(odd), t + 2 >= steps)
        )
        relays = jnp.logical_and(odd, has2)
        inner = r > 0

        def place(i):
            return jnp.where(inner, i, half - 1 - i)

        slots = [jnp.maximum(f, 2 - t) for f in range(3)]
        present = [has2, has1, None]

        frames = [
            pltpu.make_async_copy(frames_ref.at[clip], x_ref.at[clip], x_sem.at[clip])
            for clip in range(batch)
        ]
        vectors = [
            pltpu.make_async_copy(ref, scales.at[n], scale_sem.at[n])
            for n, ref in enumerate((g1_ref, n1_ref, c1_ref, g2_ref, n2_ref, c2_ref, cd_ref))
        ]
        for copy in frames + vectors:
            copy.start()

        loads = []
        for cv, k_ref in enumerate((k1_ref, k2_ref)):
            for a in range(3):
                for b in range(3):
                    for o in range(2):
                        loads.append(
                            (
                                k_ref.at[a, b],
                                weights.at[
                                    cv,
                                    pl.ds((a + o) * 3 * C, 3 * C),
                                    pl.ds((o * 3 + b) * C, C),
                                ],
                            )
                        )
        conv_loads = len(loads) // 2
        for a in range(3):
            for b in range(3):
                loads.append(
                    (
                        kd_ref.at[a, b],
                        down.at[
                            pl.ds(a * 2 * C + (C if b == 1 else 0), C),
                            pl.ds(C if b == 2 else 0, C),
                        ],
                    )
                )
        loads = [
            pltpu.make_async_copy(src, dst, k_sem.at[n])
            for n, (src, dst) in enumerate(loads)
        ]
        for load in loads:
            load.start()

        barrier = pltpu.get_barrier_semaphore()
        expected = bands - 1
        for off in range(1, bands):
            pl.semaphore_signal(
                barrier, inc=1, device_id={"rows": lax.rem(r + off, bands)}, device_id_type=MESH
            )
        for by in (-2, -1, 1, 2):
            there = jnp.logical_and(t + by >= 0, t + by < steps)
            expected = expected + there.astype(jnp.int32)

            @pl.when(there)
            def _():
                pl.semaphore_signal(
                    barrier, inc=1, device_id={"tm": t + by}, device_id_type=MESH
                )

        zero_block = jnp.zeros((3 * C, C), jnp.bfloat16)
        for cv in range(2):
            for b in range(3):
                weights[cv, 9 * C : 12 * C, b * C : (b + 1) * C] = zero_block
                weights[cv, 0 : 3 * C, (3 + b) * C : (4 + b) * C] = zero_block
        for a in range(3):
            down[(2 * a + 1) * C : (2 * a + 2) * C, C : 2 * C] = jnp.zeros((C, C), jnp.bfloat16)

        @pl.when(r == 0)
        def _():
            for cv in range(2):
                for clip in range(batch):
                    for f in range(3):
                        field[cv, clip, f, 0] = jnp.zeros((width, C), jnp.bfloat16)

        @pl.when(r == bands - 1)
        def _():
            for cv in range(2):
                for clip in range(batch):
                    for f in range(3):
                        field[cv, clip, f, height + 1] = jnp.zeros((width, C), jnp.bfloat16)
            for clip in range(batch):
                paired[clip, height] = jnp.zeros((quarter, 2 * C), jnp.bfloat16)

        def rows_of(cv, clip, slot, q):
            return field.at[cv, clip, slot, pl.ds(1 + 2 * q, 2)]

        def own2(cv, clip, q):
            return pltpu.make_async_remote_copy(
                src_ref=rows_of(cv, clip, 2, q), dst_ref=rows_of(cv, clip, 0, q),
                send_sem=own2_sem.at[cv, clip, q], recv_sem=in2_sem.at[cv, clip, q],
                device_id={"tm": t + 2}, device_id_type=MESH,
            )

        def own1(cv, clip, q):
            return pltpu.make_async_remote_copy(
                src_ref=rows_of(cv, clip, 2, q), dst_ref=rows_of(cv, clip, 1, q),
                send_sem=own1_sem.at[cv, clip, q], recv_sem=in1_sem.at[cv, clip, q],
                device_id={"tm": t + 1}, device_id_type=MESH,
            )

        def relay(cv, clip, q):
            return pltpu.make_async_remote_copy(
                src_ref=rows_of(cv, clip, 0, q), dst_ref=rows_of(cv, clip, 1, q),
                send_sem=relay_sem.at[cv, clip, q], recv_sem=in1_sem.at[cv, clip, q],
                device_id={"tm": t - 1}, device_id_type=MESH,
            )

        def edge(cv, clip, slot, way):
            src, dst, by = ((1, height + 1, -1), (height, 0, 1))[way]
            return pltpu.make_async_remote_copy(
                src_ref=field.at[cv, clip, slot, src], dst_ref=field.at[cv, clip, slot, dst],
                send_sem=edge_out.at[cv, clip, slot, way],
                recv_sem=edge_in.at[cv, clip, slot, way],
                device_id={"rows": r + by}, device_id_type=MESH,
            )

        def totals(cv, clip, off):
            return pltpu.make_async_remote_copy(
                src_ref=sums.at[cv, clip], dst_ref=others.at[cv, clip, off - 1],
                send_sem=sums_out.at[cv, clip, off - 1], recv_sem=sums_in.at[cv, clip, off - 1],
                device_id={"rows": lax.rem(r + off, bands)}, device_id_type=MESH,
            )

        def below(clip):
            return pltpu.make_async_remote_copy(
                src_ref=paired.at[clip, 0], dst_ref=paired.at[clip, height],
                send_sem=res_out.at[clip], recv_sem=res_in.at[clip],
                device_id={"rows": r - 1}, device_id_type=MESH,
            )

        def when(condition, action):
            if condition is None:
                action()
            else:
                pl.when(condition)(action)

        def both(first, second):
            return second if first is None else jnp.logical_and(first, second)

        upper = r > 0
        lower = r < bands - 1

        def start_edges(cv, clip, slot):
            when(both(present[slot], upper), lambda: edge(cv, clip, slot, 0).start())
            when(both(present[slot], lower), lambda: edge(cv, clip, slot, 1).start())

        def wait_edges(cv, clip, slot):
            when(both(present[slot], lower), lambda: edge(cv, clip, slot, 0).wait_recv())
            when(both(present[slot], upper), lambda: edge(cv, clip, slot, 1).wait_recv())

        def folded(values):
            return jnp.sum(values.reshape(width // 8, 8, C), axis=0)

        def start_totals(cv, clip, total, square):
            sums[cv, clip, 0:8] = total
            sums[cv, clip, 8:16] = square
            for off in range(1, bands):
                totals(cv, clip, off).start()

        lane = lax.broadcasted_iota(jnp.int32, (1, C), 1)
        size = C // G

        def grouped(values):
            result = values
            for k in range(1, size):
                left = pltpu.roll(values, k, 1)
                right = pltpu.roll(values, C - k, 1)
                result = result + jnp.where(lax.rem(lane, size) >= k, left, 0.0)
                result = result + jnp.where(lax.rem(lane, size) < size - k, right, 0.0)
            return result

        def constants(cv, clip):
            total = sums[cv, clip]
            for off in range(1, bands):
                totals(cv, clip, off).wait_recv()
                total = total + others[cv, clip, off - 1]
            entries = height * bands * width * size
            sum1 = jnp.broadcast_to(jnp.sum(total[0:8], axis=0, keepdims=True), (8, C))
            sum2 = jnp.broadcast_to(jnp.sum(total[8:16], axis=0, keepdims=True), (8, C))
            average = grouped(sum1)[0:1] / entries
            mean_square = grouped(sum2)[0:1] / entries
            inverse = lax.rsqrt(mean_square - average * average + EPSILON)
            return average, inverse * scales[3 * cv], scales[3 * cv + 1]

        def normalize(cv, clip, source):
            average, scale, shift = constants(cv, clip)

            def step(n, _):
                q = place(n)
                for i in range(2):
                    v = source[clip, 2 * q + i].astype(jnp.float32)
                    s = 0.5 * ((v - average) * scale + shift)
                    field[cv, clip, 2, 1 + 2 * q + i] = (s + s * jnp.tanh(s)).astype(jnp.bfloat16)
                when(sends2, lambda: own2(cv, clip, q).start())
                when(sends1, lambda: own1(cv, clip, q).start())
                return 0

            lax.fori_loop(0, half, step, 0)
            start_edges(cv, clip, 2)

        def arrive(cv, clip, n):
            q = place(n)

            @pl.when(has2)
            def _():
                own2(cv, clip, q).wait_recv()
                when(relays, lambda: relay(cv, clip, q).start())

            @pl.when(has1)
            def _():
                own1(cv, clip, q).wait_recv()

        def open_edges(cv, clip):
            early = 1 if bands <= 2 else half
            for n in range(early):
                arrive(cv, clip, n)
            for slot in (0, 1):
                start_edges(cv, clip, slot)
            for slot in (2, 0, 1):
                wait_edges(cv, clip, slot)
            return early

        def pairs(cv, clip, body, carry):
            early = open_edges(cv, clip)

            def step(n, carry):
                @pl.when(jnp.logical_and(n < half, n >= early))
                def _():
                    arrive(cv, clip, n)

                return body(place(n - 1), n, carry)

            return lax.fori_loop(1, half + 1, step, carry)

        column = lax.broadcasted_iota(jnp.int32, (width, 1), 0)

        def convolved(cv, clip, p):
            x = jnp.concatenate(
                [field[cv, clip, slots[f], 2 * p + d] for d in range(4) for f in range(3)], axis=1
            )
            dot = lambda a, b: jnp.dot(a, b, preferred_element_type=jnp.float32)
            y0 = dot(x[:, : 9 * C], weights[cv, : 9 * C, : 2 * C])
            y1 = dot(x, weights[cv, :, 2 * C : 4 * C])
            y2 = dot(x[:, 3 * C :], weights[cv, 3 * C :, 4 * C :])
            bias = scales[3 * cv + 2]

            def joined(left, middle, right):
                left = jnp.where(column >= 1, pltpu.roll(left, 1, 0), 0.0)
                right = jnp.where(column < width - 1, pltpu.roll(right, width - 1, 0), 0.0)
                return middle + left + right + bias

            return (
                joined(y0[:, :C], y0[:, C:], y1[:, :C]),
                joined(y1[:, C:], y2[:, :C], y2[:, C:]),
            )

        def conv_one(clip):
            def step(p, n, carry):
                total, square = carry
                for i, y in enumerate(convolved(0, clip, p)):
                    y = y.astype(jnp.bfloat16)
                    hidden[clip, 2 * p + i] = y
                    y = y.astype(jnp.float32)
                    total = total + folded(y)
                    square = square + folded(y * y)
                return total, square

            zero = jnp.zeros((8, C), jnp.float32)
            start_totals(1, clip, *pairs(0, clip, step, (zero, zero)))

        def conv_two(clip):
            def step(p, n, _):
                for i, y in enumerate(convolved(1, clip, p)):
                    y = y + x_ref[clip, 2 * p + i].astype(jnp.float32)
                    spread[i] = y.astype(jnp.bfloat16).astype(jnp.float32)
                    even = spread[i, pl.ds(0, quarter, stride=2), :]
                    uneven = spread[i, pl.ds(1, quarter, stride=2), :]
                    paired[clip, 2 * p + i] = jnp.concatenate(
                        [even.astype(jnp.bfloat16), uneven.astype(jnp.bfloat16)], axis=1
                    )

                @pl.when(jnp.logical_and(upper, n == 1))
                def _():
                    below(clip).start()

                return 0

            pairs(1, clip, step, 0)

        narrow = lax.broadcasted_iota(jnp.int32, (quarter, 1), 0)

        def downsample(clip):
            when(lower, lambda: below(clip).wait_recv())
            x = jnp.concatenate(
                [
                    jnp.concatenate([paired[clip, 2 * i + a] for a in range(3)], axis=1)
                    for i in range(half)
                ],
                axis=0,
            )
            y = jnp.dot(x, down[...], preferred_element_type=jnp.float32)
            for i in range(half):
                rows = y[i * quarter : (i + 1) * quarter]
                right = pltpu.roll(rows[:, C:], quarter - 1, 0)
                rows = rows[:, :C] + jnp.where(narrow < quarter - 1, right, 0.0) + scales[6]
                out_ref[clip, i] = rows.astype(jnp.bfloat16)

        for clip in range(batch):
            def gather(i, carry):
                v = x_ref[clip, i].astype(jnp.float32)
                return carry[0] + folded(v), carry[1] + folded(v * v)

            zero = jnp.zeros((8, C), jnp.float32)
            frames[clip].wait()
            found = lax.fori_loop(0, height, gather, (zero, zero))
            if clip == 0:
                pl.semaphore_wait(barrier, expected)
            start_totals(0, clip, *found)
        for vector in vectors:
            vector.wait()
        for clip in range(batch):
            normalize(0, clip, x_ref)
        for load in loads[:conv_loads]:
            load.wait()
        for clip in range(batch):
            conv_one(clip)
            normalize(1, clip, hidden)
        for load in loads[conv_loads:]:
            load.wait()
        for clip in range(batch):
            conv_two(clip)
            downsample(clip)

        for cv in range(2):
            for clip in range(batch):
                def leave(q, _):
                    when(sends2, lambda: own2(cv, clip, q).wait_send())
                    when(sends1, lambda: own1(cv, clip, q).wait_send())
                    when(relays, lambda: relay(cv, clip, q).wait_send())
                    return 0

                lax.fori_loop(0, half, leave, 0)
                for slot in range(3):
                    when(both(present[slot], upper), lambda: edge(cv, clip, slot, 0).wait_send())
                    when(both(present[slot], lower), lambda: edge(cv, clip, slot, 1).wait_send())
                for off in range(1, bands):
                    totals(cv, clip, off).wait_send()
        for clip in range(batch):
            when(upper, lambda: below(clip).wait_send())

    vmem = pl.BlockSpec(memory_space=pltpu.VMEM)
    hbm = pl.BlockSpec(memory_space=pl.ANY)
    dma = pltpu.SemaphoreType.DMA
    return pl.pallas_call(
        kernel,
        out_shape=jax.ShapeDtypeStruct((batch, half, quarter, C), jnp.bfloat16),
        in_specs=[hbm] * 11,
        out_specs=vmem,
        scratch_shapes=[
            pltpu.VMEM((batch, height, width, C), jnp.bfloat16),
            pltpu.VMEM((7, 1, C), jnp.float32),
            pltpu.VMEM((2, batch, 3, height + 2, width, C), jnp.bfloat16),
            pltpu.VMEM((2, 12 * C, 6 * C), jnp.bfloat16),
            pltpu.VMEM((6 * C, 2 * C), jnp.bfloat16),
            pltpu.VMEM((batch, height, width, C), jnp.bfloat16),
            pltpu.VMEM((batch, height + 1, quarter, 2 * C), jnp.bfloat16),
            pltpu.VMEM((2, width, C), jnp.float32),
            pltpu.VMEM((2, batch, 16, C), jnp.float32),
            pltpu.VMEM((2, batch, max(bands - 1, 1), 16, C), jnp.float32),
            dma((batch,)),
            dma((7,)),
            dma((45,)),
            dma((2, batch, half)),
            dma((2, batch, half)),
            dma((2, batch, half)),
            dma((2, batch, half)),
            dma((2, batch, half)),
            dma((2, batch, 3, 2)),
            dma((2, batch, 3, 2)),
            dma((2, batch, max(bands - 1, 1))),
            dma((2, batch, max(bands - 1, 1))),
            dma((batch,)),
            dma((batch,)),
        ],
        compiler_params=pltpu.CompilerParams(
            collective_id=0, has_side_effects=True, vmem_limit_bytes=60 * 1024 * 1024
        ),
    )


def solution(mesh):
    steps, bands = mesh.shape["tm"], mesh.shape["rows"]

    def local(
        frames_in,
        gain_one,
        norm_bias_one,
        kernel_one,
        bias_one,
        gain_two,
        norm_bias_two,
        kernel_two,
        bias_two,
        kernel_down,
        bias_down,
    ):
        inputs = frames_in[:, 0]
        batch, height, width, channels = inputs.shape
        vectors = [
            v.reshape(1, channels)
            for v in (
                gain_one, norm_bias_one, bias_one, gain_two, norm_bias_two, bias_two, bias_down
            )
        ]
        wide = (3, 3, 3 * channels, channels)
        call = build(batch, height, width, channels, steps, bands)
        result = call(
            inputs, *vectors, kernel_one.reshape(wide), kernel_two.reshape(wide), kernel_down
        )
        return result[:, None]

    placed = (P("groups", "tm", "rows", None, None),) + (P(),) * 10
    return jax.shard_map(
        local,
        mesh=mesh,
        in_specs=placed,
        out_specs=P("groups", "tm", "rows", None, None),
        check_vma=False,
    )
```

```python
import jax
import jax.numpy as jnp
from jax import lax
from jax.experimental import pallas as pl
from jax.experimental.pallas import tpu as pltpu
from jax.sharding import PartitionSpec as P

G = 32


EPSILON = 1e-06

MESH = pl.DeviceIdType.MESH


def build(batch, height, width, channels, steps, bands):
    half = height // 2
    quarter = width // 2
    C = channels

    def kernel(
        frames_ref, g1_ref, n1_ref, c1_ref, g2_ref, n2_ref, c2_ref, cd_ref,
        k1_ref, k2_ref, kd_ref, out_ref,
        x_ref, scales, raw, whole, arrived, settled, field, weights, down, hidden, paired, spread, sums, others,
        x_sem, scale_sem, k_sem, own2_sem, own1_sem, relay_sem, in2_sem, in1_sem,
        whole2_sem, whole1_sem, whole_relay_sem, whole_in, edge_out, edge_in, sums_out, sums_in, res_out, res_in,
    ):
        t = lax.axis_index("tm")
        r = lax.axis_index("rows")
        has1 = t >= 1
        has2 = t >= 2
        odd = lax.rem(t, 2) == 1
        sends2 = t + 2 < steps
        sends1 = jnp.logical_and(
            t + 1 < steps, jnp.logical_or(jnp.logical_not(odd), t + 2 >= steps)
        )
        relays = jnp.logical_and(odd, has2)
        inner = r > 0

        def place(i):
            return jnp.where(inner, i, half - 1 - i)

        def row_at(n, i):
            return jnp.where(inner, 2 * n + i, height - 1 - 2 * n - i)

        slots = [jnp.maximum(f, 2 - t) for f in range(3)]
        present = [has2, has1, None]

        barrier = pltpu.get_barrier_semaphore()
        expected = bands - 1
        for off in range(1, bands):
            pl.semaphore_signal(
                barrier, inc=1, device_id={"rows": lax.rem(r + off, bands)}, device_id_type=MESH
            )
        for by in (-2, -1, 1, 2):
            there = jnp.logical_and(t + by >= 0, t + by < steps)
            expected = expected + there.astype(jnp.int32)

            @pl.when(there)
            def _():
                pl.semaphore_signal(
                    barrier, inc=1, device_id={"tm": t + by}, device_id_type=MESH
                )

        frames = [
            pltpu.make_async_copy(frames_ref.at[clip], x_ref.at[clip], x_sem.at[clip])
            for clip in range(batch)
        ]
        vectors = [
            pltpu.make_async_copy(ref, scales.at[n], scale_sem.at[n])
            for n, ref in enumerate((g1_ref, n1_ref, c1_ref, g2_ref, n2_ref, c2_ref, cd_ref))
        ]
        for copy in frames + vectors:
            copy.start()

        loads = []
        for cv, k_ref in enumerate((k1_ref, k2_ref)):
            for a in range(3):
                for b in range(3):
                    for o in range(2):
                        loads.append(
                            (
                                k_ref.at[a, b],
                                weights.at[
                                    cv,
                                    pl.ds((a + o) * 3 * C, 3 * C),
                                    pl.ds((o * 3 + b) * C, C),
                                ],
                            )
                        )
        conv_loads = len(loads) // 2
        for a in range(3):
            for b in range(3):
                loads.append(
                    (
                        kd_ref.at[a, b],
                        down.at[
                            pl.ds(a * 2 * C + (C if b == 1 else 0), C),
                            pl.ds(C if b == 2 else 0, C),
                        ],
                    )
                )
        loads = [
            pltpu.make_async_copy(src, dst, k_sem.at[n])
            for n, (src, dst) in enumerate(loads)
        ]
        for load in loads:
            load.start()

        zero_block = jnp.zeros((3 * C, C), jnp.bfloat16)
        for cv in range(2):
            for b in range(3):
                weights[cv, 9 * C : 12 * C, b * C : (b + 1) * C] = zero_block
                weights[cv, 0 : 3 * C, (3 + b) * C : (4 + b) * C] = zero_block
        for a in range(3):
            down[(2 * a + 1) * C : (2 * a + 2) * C, C : 2 * C] = jnp.zeros((C, C), jnp.bfloat16)

        @pl.when(r == 0)
        def _():
            for cv in range(2):
                for clip in range(batch):
                    for f in range(3):
                        field[cv, clip, f, 0] = jnp.zeros((width, C), jnp.bfloat16)

        @pl.when(r == bands - 1)
        def _():
            for cv in range(2):
                for clip in range(batch):
                    for f in range(3):
                        field[cv, clip, f, height + 1] = jnp.zeros((width, C), jnp.bfloat16)
            for clip in range(batch):
                paired[clip, height] = jnp.zeros((quarter, 2 * C), jnp.bfloat16)

        def landing(cv, clip, slot, row):
            if cv == 0:
                return raw.at[clip, slot, row]
            return field.at[cv, clip, slot, row + 1]

        def leaving(cv, clip, row):
            if cv == 0:
                return frames_ref.at[clip, row]
            return field.at[cv, clip, 2, row + 1]

        def own2(cv, clip, q):
            return pltpu.make_async_remote_copy(
                src_ref=leaving(cv, clip, q), dst_ref=landing(cv, clip, 0, q),
                send_sem=own2_sem.at[cv, clip, q], recv_sem=in2_sem.at[cv, clip, q],
                device_id={"tm": t + 2}, device_id_type=MESH,
            )

        def own1(cv, clip, q):
            return pltpu.make_async_remote_copy(
                src_ref=leaving(cv, clip, q), dst_ref=landing(cv, clip, 1, q),
                send_sem=own1_sem.at[cv, clip, q], recv_sem=in1_sem.at[cv, clip, q],
                device_id={"tm": t + 1}, device_id_type=MESH,
            )

        def relay(cv, clip, q):
            return pltpu.make_async_remote_copy(
                src_ref=landing(cv, clip, 0, q), dst_ref=landing(cv, clip, 1, q),
                send_sem=relay_sem.at[cv, clip, q], recv_sem=in1_sem.at[cv, clip, q],
                device_id={"tm": t - 1}, device_id_type=MESH,
            )

        def whole2(clip):
            return pltpu.make_async_remote_copy(
                src_ref=whole.at[clip], dst_ref=arrived.at[clip, 0],
                send_sem=whole2_sem.at[clip], recv_sem=whole_in.at[clip, 0],
                device_id={"tm": t + 2}, device_id_type=MESH,
            )

        def whole1(clip):
            return pltpu.make_async_remote_copy(
                src_ref=whole.at[clip], dst_ref=arrived.at[clip, 1],
                send_sem=whole1_sem.at[clip], recv_sem=whole_in.at[clip, 1],
                device_id={"tm": t + 1}, device_id_type=MESH,
            )

        def whole_relay(clip):
            return pltpu.make_async_remote_copy(
                src_ref=arrived.at[clip, 0], dst_ref=arrived.at[clip, 1],
                send_sem=whole_relay_sem.at[clip], recv_sem=whole_in.at[clip, 1],
                device_id={"tm": t - 1}, device_id_type=MESH,
            )

        def edge(cv, clip, slot, way):
            src, dst, by = ((1, height + 1, -1), (height, 0, 1))[way]
            return pltpu.make_async_remote_copy(
                src_ref=field.at[cv, clip, slot, src], dst_ref=field.at[cv, clip, slot, dst],
                send_sem=edge_out.at[cv, clip, slot, way],
                recv_sem=edge_in.at[cv, clip, slot, way],
                device_id={"rows": r + by}, device_id_type=MESH,
            )

        def totals(cv, clip, off):
            return pltpu.make_async_remote_copy(
                src_ref=sums.at[cv, clip], dst_ref=others.at[cv, clip, off - 1],
                send_sem=sums_out.at[cv, clip, off - 1], recv_sem=sums_in.at[cv, clip, off - 1],
                device_id={"rows": lax.rem(r + off, bands)}, device_id_type=MESH,
            )

        def below(clip):
            return pltpu.make_async_remote_copy(
                src_ref=paired.at[clip, 0], dst_ref=paired.at[clip, height],
                send_sem=res_out.at[clip], recv_sem=res_in.at[clip],
                device_id={"rows": r - 1}, device_id_type=MESH,
            )

        def when(condition, action):
            if condition is None:
                action()
            else:
                pl.when(condition)(action)

        def both(first, second):
            return second if first is None else jnp.logical_and(first, second)

        upper = r > 0
        lower = r < bands - 1

        def start_edges(cv, clip, slot):
            when(both(present[slot], upper), lambda: edge(cv, clip, slot, 0).start())
            when(both(present[slot], lower), lambda: edge(cv, clip, slot, 1).start())

        def wait_edges(cv, clip, slot):
            when(both(present[slot], lower), lambda: edge(cv, clip, slot, 0).wait_recv())
            when(both(present[slot], upper), lambda: edge(cv, clip, slot, 1).wait_recv())

        def folded(values):
            return jnp.sum(values.reshape(width // 8, 8, C), axis=0)

        def start_totals(cv, clip, total, square):
            sums[cv, clip, 0:8] = total
            sums[cv, clip, 8:16] = square
            for off in range(1, bands):
                totals(cv, clip, off).start()

        lane = lax.broadcasted_iota(jnp.int32, (1, C), 1)
        size = C // G

        def grouped(values):
            result = values
            for k in range(1, size):
                left = pltpu.roll(values, k, 1)
                right = pltpu.roll(values, C - k, 1)
                result = result + jnp.where(lax.rem(lane, size) >= k, left, 0.0)
                result = result + jnp.where(lax.rem(lane, size) < size - k, right, 0.0)
            return result

        def summed(cv, clip):
            total = sums[cv, clip]
            for off in range(1, bands):
                totals(cv, clip, off).wait_recv()
                total = total + others[cv, clip, off - 1]
            return total

        def constants(cv, total):
            entries = height * bands * width * size
            sum1 = jnp.broadcast_to(jnp.sum(total[0:8], axis=0, keepdims=True), (8, C))
            sum2 = jnp.broadcast_to(jnp.sum(total[8:16], axis=0, keepdims=True), (8, C))
            average = grouped(sum1)[0:1] / entries
            mean_square = grouped(sum2)[0:1] / entries
            inverse = lax.rsqrt(mean_square - average * average + EPSILON)
            return average, inverse * scales[3 * cv]

        def normed(cv, values, average, scale):
            s = 0.5 * ((values.astype(jnp.float32) - average) * scale + scales[3 * cv + 1])
            return (s + s * jnp.tanh(s)).astype(jnp.bfloat16)

        def send(cv, clip, row):
            when(sends2, lambda: own2(cv, clip, row).start())
            when(sends1, lambda: own1(cv, clip, row).start())

        def normalize(cv, clip, source, total):
            average, scale = constants(cv, total)

            def step(n, _):
                for i in range(2):
                    row = row_at(n, i)
                    field[cv, clip, 2, row + 1] = normed(cv, source[clip, row], average, scale)
                    if cv == 1:
                        send(cv, clip, row)
                return 0

            lax.fori_loop(0, half, step, 0)
            start_edges(cv, clip, 2)

        def land(cv, clip, n):
            @pl.when(has2)
            def _():
                for i in range(2):
                    row = row_at(n, i)
                    own2(cv, clip, row).wait_recv()
                    when(relays, lambda: relay(cv, clip, row).start())

        def settle(cv, clip, n):
            def take(slot):
                for i in range(2):
                    row = row_at(n, i)
                    if slot == 1:
                        own1(cv, clip, row).wait_recv()
                    if cv == 0:
                        field[cv, clip, slot, row + 1] = normed(
                            cv, raw[clip, slot, row], settled[slot, 0], settled[slot, 1]
                        )

            for slot in range(2):
                when(present[slot], lambda: take(slot))

        def learn(clip):
            def take(slot):
                whole_in_copy = (whole2, whole1)[slot](clip)
                whole_in_copy.wait_recv()
                if slot == 0:
                    when(relays, lambda: whole_relay(clip).start())
                settled[slot, 0], settled[slot, 1] = constants(0, arrived[clip, slot])

            for slot in range(2):
                when(present[slot], lambda: take(slot))

        lead = min(2, half)

        def open_edges(cv, clip):
            early = 1 if bands <= 2 else half
            ahead = max(early, lead if cv == 0 else 1)
            for n in range(ahead):
                land(cv, clip, n)
            if cv == 0:
                learn(clip)
            for n in range(early):
                settle(cv, clip, n)
            for slot in (0, 1):
                start_edges(cv, clip, slot)
            for slot in (2, 0, 1):
                wait_edges(cv, clip, slot)
            return early, ahead

        def pairs(cv, clip, body, carry):
            early, ahead = open_edges(cv, clip)

            def step(n, carry):
                @pl.when(jnp.logical_and(n < half, n >= ahead))
                def _():
                    land(cv, clip, n)

                @pl.when(jnp.logical_and(n < half, n >= early))
                def _():
                    settle(cv, clip, n)

                return body(place(n - 1), n, carry)

            return lax.fori_loop(1, half + 1, step, carry)

        column = lax.broadcasted_iota(jnp.int32, (width, 1), 0)

        def convolved(cv, clip, p):
            x = jnp.concatenate(
                [field[cv, clip, slots[f], 2 * p + d] for d in range(4) for f in range(3)], axis=1
            )
            dot = lambda a, b: jnp.dot(a, b, preferred_element_type=jnp.float32)
            y0 = dot(x[:, : 9 * C], weights[cv, : 9 * C, : 2 * C])
            y1 = dot(x, weights[cv, :, 2 * C : 4 * C])
            y2 = dot(x[:, 3 * C :], weights[cv, 3 * C :, 4 * C :])
            bias = scales[3 * cv + 2]

            def joined(left, middle, right):
                left = jnp.where(column >= 1, pltpu.roll(left, 1, 0), 0.0)
                right = jnp.where(column < width - 1, pltpu.roll(right, width - 1, 0), 0.0)
                return middle + left + right + bias

            return (
                joined(y0[:, :C], y0[:, C:], y1[:, :C]),
                joined(y1[:, C:], y2[:, :C], y2[:, C:]),
            )

        def conv_one(clip):
            def step(p, n, carry):
                total, square = carry
                for i, y in enumerate(convolved(0, clip, p)):
                    y = y.astype(jnp.bfloat16)
                    hidden[clip, 2 * p + i] = y
                    y = y.astype(jnp.float32)
                    total = total + folded(y)
                    square = square + folded(y * y)
                return total, square

            zero = jnp.zeros((8, C), jnp.float32)
            start_totals(1, clip, *pairs(0, clip, step, (zero, zero)))

        def conv_two(clip):
            def step(p, n, _):
                for i, y in enumerate(convolved(1, clip, p)):
                    y = y + x_ref[clip, 2 * p + i].astype(jnp.float32)
                    spread[i] = y.astype(jnp.bfloat16).astype(jnp.float32)
                    even = spread[i, pl.ds(0, quarter, stride=2), :]
                    uneven = spread[i, pl.ds(1, quarter, stride=2), :]
                    paired[clip, 2 * p + i] = jnp.concatenate(
                        [even.astype(jnp.bfloat16), uneven.astype(jnp.bfloat16)], axis=1
                    )

                @pl.when(jnp.logical_and(upper, n == 1))
                def _():
                    below(clip).start()

                return 0

            pairs(1, clip, step, 0)

        narrow = lax.broadcasted_iota(jnp.int32, (quarter, 1), 0)

        def downsample(clip):
            when(lower, lambda: below(clip).wait_recv())
            x = jnp.concatenate(
                [
                    jnp.concatenate([paired[clip, 2 * i + a] for a in range(3)], axis=1)
                    for i in range(half)
                ],
                axis=0,
            )
            y = jnp.dot(x, down[...], preferred_element_type=jnp.float32)
            for i in range(half):
                rows = y[i * quarter : (i + 1) * quarter]
                right = pltpu.roll(rows[:, C:], quarter - 1, 0)
                rows = rows[:, :C] + jnp.where(narrow < quarter - 1, right, 0.0) + scales[6]
                out_ref[clip, i] = rows.astype(jnp.bfloat16)

        def send_frames(clip, first, last):
            def step(n, _):
                for i in range(2):
                    send(0, clip, row_at(n, i))
                return 0

            lax.fori_loop(first, last, step, 0)

        pl.semaphore_wait(barrier, expected)
        send_frames(0, 0, lead)
        for clip in range(batch):
            def gather(i, carry):
                v = x_ref[clip, i].astype(jnp.float32)
                return carry[0] + folded(v), carry[1] + folded(v * v)

            zero = jnp.zeros((8, C), jnp.float32)
            frames[clip].wait()
            start_totals(0, clip, *lax.fori_loop(0, height, gather, (zero, zero)))
        for clip in range(batch):
            if clip > 0:
                send_frames(clip, 0, lead)
            whole[clip] = summed(0, clip)
            when(sends2, lambda: whole2(clip).start())
            when(sends1, lambda: whole1(clip).start())
            send_frames(clip, lead, half)
        for vector in vectors:
            vector.wait()
        for clip in range(batch):
            normalize(0, clip, x_ref, whole[clip])
        for load in loads[:conv_loads]:
            load.wait()
        for clip in range(batch):
            conv_one(clip)
            normalize(1, clip, hidden, summed(1, clip))
        for load in loads[conv_loads:]:
            load.wait()
        for clip in range(batch):
            conv_two(clip)
            downsample(clip)

        for cv in range(2):
            for clip in range(batch):
                def leave(q, _):
                    when(sends2, lambda: own2(cv, clip, q).wait_send())
                    when(sends1, lambda: own1(cv, clip, q).wait_send())
                    when(relays, lambda: relay(cv, clip, q).wait_send())
                    return 0

                lax.fori_loop(0, height, leave, 0)
                for slot in range(3):
                    when(both(present[slot], upper), lambda: edge(cv, clip, slot, 0).wait_send())
                    when(both(present[slot], lower), lambda: edge(cv, clip, slot, 1).wait_send())
                for off in range(1, bands):
                    totals(cv, clip, off).wait_send()
        for clip in range(batch):
            when(upper, lambda: below(clip).wait_send())
            when(sends2, lambda: whole2(clip).wait_send())
            when(sends1, lambda: whole1(clip).wait_send())
            when(relays, lambda: whole_relay(clip).wait_send())

    vmem = pl.BlockSpec(memory_space=pltpu.VMEM)
    hbm = pl.BlockSpec(memory_space=pltpu.HBM)
    dma = pltpu.SemaphoreType.DMA
    return pl.pallas_call(
        kernel,
        out_shape=jax.ShapeDtypeStruct((batch, half, quarter, C), jnp.bfloat16),
        in_specs=[hbm] * 11,
        out_specs=vmem,
        scratch_shapes=[
            pltpu.VMEM((batch, height, width, C), jnp.bfloat16),
            pltpu.VMEM((7, 1, C), jnp.float32),
            pltpu.VMEM((batch, 2, height, width, C), jnp.bfloat16),
            pltpu.VMEM((batch, 16, C), jnp.float32),
            pltpu.VMEM((batch, 2, 16, C), jnp.float32),
            pltpu.VMEM((2, 2, 1, C), jnp.float32),
            pltpu.VMEM((2, batch, 3, height + 2, width, C), jnp.bfloat16),
            pltpu.VMEM((2, 12 * C, 6 * C), jnp.bfloat16),
            pltpu.VMEM((6 * C, 2 * C), jnp.bfloat16),
            pltpu.VMEM((batch, height, width, C), jnp.bfloat16),
            pltpu.VMEM((batch, height + 1, quarter, 2 * C), jnp.bfloat16),
            pltpu.VMEM((2, width, C), jnp.float32),
            pltpu.VMEM((2, batch, 16, C), jnp.float32),
            pltpu.VMEM((2, batch, max(bands - 1, 1), 16, C), jnp.float32),
            dma((batch,)),
            dma((7,)),
            dma((45,)),
            dma((2, batch, height)),
            dma((2, batch, height)),
            dma((2, batch, height)),
            dma((2, batch, height)),
            dma((2, batch, height)),
            dma((batch,)),
            dma((batch,)),
            dma((batch,)),
            dma((batch, 2)),
            dma((2, batch, 3, 2)),
            dma((2, batch, 3, 2)),
            dma((2, batch, max(bands - 1, 1))),
            dma((2, batch, max(bands - 1, 1))),
            dma((batch,)),
            dma((batch,)),
        ],
        compiler_params=pltpu.CompilerParams(
            collective_id=0, has_side_effects=True, vmem_limit_bytes=60 * 1024 * 1024
        ),
    )


def solution(mesh):
    steps, bands = mesh.shape["tm"], mesh.shape["rows"]

    def local(
        frames_in,
        gain_one,
        norm_bias_one,
        kernel_one,
        bias_one,
        gain_two,
        norm_bias_two,
        kernel_two,
        bias_two,
        kernel_down,
        bias_down,
    ):
        inputs = frames_in[:, 0]
        batch, height, width, channels = inputs.shape
        vectors = [
            v.reshape(1, channels)
            for v in (
                gain_one, norm_bias_one, bias_one, gain_two, norm_bias_two, bias_two, bias_down
            )
        ]
        wide = (3, 3, 3 * channels, channels)
        call = build(batch, height, width, channels, steps, bands)
        result = call(
            inputs, *vectors, kernel_one.reshape(wide), kernel_two.reshape(wide), kernel_down
        )
        return result[:, None]

    placed = (P("groups", "tm", "rows", None, None),) + (P(),) * 10
    return jax.shard_map(
        local,
        mesh=mesh,
        in_specs=placed,
        out_specs=P("groups", "tm", "rows", None, None),
        check_vma=False,
    )
```

```python
import jax
import jax.numpy as jnp
from jax import lax
from jax.experimental import pallas as pl
from jax.experimental.pallas import tpu as pltpu
from jax.sharding import PartitionSpec as P

G = 32


EPSILON = 1e-06

MESH = pl.DeviceIdType.MESH


def build(batch, height, width, channels, steps, bands):
    half = height // 2
    quarter = width // 2
    C = channels

    def kernel(
        frames_ref, g1_ref, n1_ref, c1_ref, g2_ref, n2_ref, c2_ref, cd_ref,
        k1_ref, k2_ref, kd_ref, out_ref,
        x_ref, scales, raw, whole, arrived, settled, field, weights, down, hidden, paired, spread, sums, others,
        x_sem, scale_sem, k_sem, own2_sem, own1_sem, relay_sem, in2_sem, in1_sem,
        whole2_sem, whole1_sem, whole_relay_sem, whole_in, edge_out, edge_in, sums_out, sums_in, res_out, res_in,
    ):
        t = lax.axis_index("tm")
        r = lax.axis_index("rows")
        has1 = t >= 1
        has2 = t >= 2
        odd = lax.rem(t, 2) == 1
        sends2 = t + 2 < steps
        sends1 = jnp.logical_and(
            t + 1 < steps, jnp.logical_or(jnp.logical_not(odd), t + 2 >= steps)
        )
        relays = jnp.logical_and(odd, has2)
        inner = r > 0

        def place(i):
            return jnp.where(inner, i, half - 1 - i)

        def row_at(n, i):
            return jnp.where(inner, 2 * n + i, height - 1 - 2 * n - i)

        slots = [jnp.maximum(f, 2 - t) for f in range(3)]
        present = [has2, has1, None]

        barrier = pltpu.get_barrier_semaphore()
        expected = bands - 1
        for off in range(1, bands):
            pl.semaphore_signal(
                barrier, inc=1, device_id={"rows": lax.rem(r + off, bands)}, device_id_type=MESH
            )
        for by in (-2, -1, 1, 2):
            there = jnp.logical_and(t + by >= 0, t + by < steps)
            expected = expected + there.astype(jnp.int32)

            @pl.when(there)
            def _():
                pl.semaphore_signal(
                    barrier, inc=1, device_id={"tm": t + by}, device_id_type=MESH
                )

        frames = [
            pltpu.make_async_copy(frames_ref.at[clip], x_ref.at[clip], x_sem.at[clip])
            for clip in range(batch)
        ]
        vectors = [
            pltpu.make_async_copy(ref, scales.at[n], scale_sem.at[n])
            for n, ref in enumerate((g1_ref, n1_ref, c1_ref, g2_ref, n2_ref, c2_ref, cd_ref))
        ]
        for copy in frames + vectors:
            copy.start()

        loads = []
        for cv, k_ref in enumerate((k1_ref, k2_ref)):
            for a in range(3):
                for b in range(3):
                    for o in range(2):
                        loads.append(
                            (
                                k_ref.at[a, b],
                                weights.at[
                                    cv,
                                    pl.ds((a + o) * 3 * C, 3 * C),
                                    pl.ds((o * 3 + b) * C, C),
                                ],
                            )
                        )
        conv_loads = len(loads) // 2
        for a in range(3):
            for b in range(3):
                loads.append(
                    (
                        kd_ref.at[a, b],
                        down.at[
                            pl.ds(a * 2 * C + (C if b == 1 else 0), C),
                            pl.ds(C if b == 2 else 0, C),
                        ],
                    )
                )
        loads = [
            pltpu.make_async_copy(src, dst, k_sem.at[n])
            for n, (src, dst) in enumerate(loads)
        ]
        for load in loads:
            load.start()

        zero_block = jnp.zeros((3 * C, C), jnp.bfloat16)
        for cv in range(2):
            for b in range(3):
                weights[cv, 9 * C : 12 * C, b * C : (b + 1) * C] = zero_block
                weights[cv, 0 : 3 * C, (3 + b) * C : (4 + b) * C] = zero_block
        for a in range(3):
            down[(2 * a + 1) * C : (2 * a + 2) * C, C : 2 * C] = jnp.zeros((C, C), jnp.bfloat16)

        @pl.when(r == 0)
        def _():
            for cv in range(2):
                for clip in range(batch):
                    for f in range(3):
                        field[cv, clip, f, 0] = jnp.zeros((width, C), jnp.bfloat16)

        @pl.when(r == bands - 1)
        def _():
            for cv in range(2):
                for clip in range(batch):
                    for f in range(3):
                        field[cv, clip, f, height + 1] = jnp.zeros((width, C), jnp.bfloat16)
            for clip in range(batch):
                paired[clip, height] = jnp.zeros((quarter, 2 * C), jnp.bfloat16)

        def landing(cv, clip, slot, row):
            if cv == 0:
                return raw.at[clip, slot, row]
            return field.at[cv, clip, slot, row + 1]

        def leaving(cv, clip, row):
            if cv == 0:
                return frames_ref.at[clip, row]
            return field.at[cv, clip, 2, row + 1]

        def own2(cv, clip, q):
            return pltpu.make_async_remote_copy(
                src_ref=leaving(cv, clip, q), dst_ref=landing(cv, clip, 0, q),
                send_sem=own2_sem.at[cv, clip, q], recv_sem=in2_sem.at[cv, clip, q],
                device_id={"tm": t + 2}, device_id_type=MESH,
            )

        def own1(cv, clip, q):
            return pltpu.make_async_remote_copy(
                src_ref=leaving(cv, clip, q), dst_ref=landing(cv, clip, 1, q),
                send_sem=own1_sem.at[cv, clip, q], recv_sem=in1_sem.at[cv, clip, q],
                device_id={"tm": t + 1}, device_id_type=MESH,
            )

        def relay(cv, clip, q):
            return pltpu.make_async_remote_copy(
                src_ref=landing(cv, clip, 0, q), dst_ref=landing(cv, clip, 1, q),
                send_sem=relay_sem.at[cv, clip, q], recv_sem=in1_sem.at[cv, clip, q],
                device_id={"tm": t - 1}, device_id_type=MESH,
            )

        def whole2(clip):
            return pltpu.make_async_remote_copy(
                src_ref=whole.at[clip], dst_ref=arrived.at[clip, 0],
                send_sem=whole2_sem.at[clip], recv_sem=whole_in.at[clip, 0],
                device_id={"tm": t + 2}, device_id_type=MESH,
            )

        def whole1(clip):
            return pltpu.make_async_remote_copy(
                src_ref=whole.at[clip], dst_ref=arrived.at[clip, 1],
                send_sem=whole1_sem.at[clip], recv_sem=whole_in.at[clip, 1],
                device_id={"tm": t + 1}, device_id_type=MESH,
            )

        def whole_relay(clip):
            return pltpu.make_async_remote_copy(
                src_ref=arrived.at[clip, 0], dst_ref=arrived.at[clip, 1],
                send_sem=whole_relay_sem.at[clip], recv_sem=whole_in.at[clip, 1],
                device_id={"tm": t - 1}, device_id_type=MESH,
            )

        def edge(cv, clip, slot, way):
            src, dst, by = ((1, height + 1, -1), (height, 0, 1))[way]
            return pltpu.make_async_remote_copy(
                src_ref=field.at[cv, clip, slot, src], dst_ref=field.at[cv, clip, slot, dst],
                send_sem=edge_out.at[cv, clip, slot, way],
                recv_sem=edge_in.at[cv, clip, slot, way],
                device_id={"rows": r + by}, device_id_type=MESH,
            )

        def totals(cv, clip, off):
            return pltpu.make_async_remote_copy(
                src_ref=sums.at[cv, clip], dst_ref=others.at[cv, clip, off - 1],
                send_sem=sums_out.at[cv, clip, off - 1], recv_sem=sums_in.at[cv, clip, off - 1],
                device_id={"rows": lax.rem(r + off, bands)}, device_id_type=MESH,
            )

        def below(clip):
            return pltpu.make_async_remote_copy(
                src_ref=paired.at[clip, 0], dst_ref=paired.at[clip, height],
                send_sem=res_out.at[clip], recv_sem=res_in.at[clip],
                device_id={"rows": r - 1}, device_id_type=MESH,
            )

        def when(condition, action):
            if condition is None:
                action()
            else:
                pl.when(condition)(action)

        def both(first, second):
            return second if first is None else jnp.logical_and(first, second)

        upper = r > 0
        lower = r < bands - 1

        def start_edges(cv, clip, slot):
            when(both(present[slot], upper), lambda: edge(cv, clip, slot, 0).start())
            when(both(present[slot], lower), lambda: edge(cv, clip, slot, 1).start())

        def wait_edges(cv, clip, slot):
            when(both(present[slot], lower), lambda: edge(cv, clip, slot, 0).wait_recv())
            when(both(present[slot], upper), lambda: edge(cv, clip, slot, 1).wait_recv())

        def folded(values):
            return jnp.sum(values.reshape(width // 8, 8, C), axis=0)

        def start_totals(cv, clip, total, square):
            sums[cv, clip, 0:8] = total
            sums[cv, clip, 8:16] = square
            for off in range(1, bands):
                totals(cv, clip, off).start()

        lane = lax.broadcasted_iota(jnp.int32, (1, C), 1)
        size = C // G

        def grouped(values):
            result = values
            for k in range(1, size):
                left = pltpu.roll(values, k, 1)
                right = pltpu.roll(values, C - k, 1)
                result = result + jnp.where(lax.rem(lane, size) >= k, left, 0.0)
                result = result + jnp.where(lax.rem(lane, size) < size - k, right, 0.0)
            return result

        def summed(cv, clip):
            total = sums[cv, clip]
            for off in range(1, bands):
                totals(cv, clip, off).wait_recv()
                total = total + others[cv, clip, off - 1]
            return total

        def constants(cv, total):
            entries = height * bands * width * size
            sum1 = jnp.broadcast_to(jnp.sum(total[0:8], axis=0, keepdims=True), (8, C))
            sum2 = jnp.broadcast_to(jnp.sum(total[8:16], axis=0, keepdims=True), (8, C))
            average = grouped(sum1)[0:1] / entries
            mean_square = grouped(sum2)[0:1] / entries
            inverse = lax.rsqrt(mean_square - average * average + EPSILON)
            return average, inverse * scales[3 * cv]

        def normed(cv, values, average, scale):
            s = 0.5 * ((values.astype(jnp.float32) - average) * scale + scales[3 * cv + 1])
            return (s + s * jnp.tanh(s)).astype(jnp.bfloat16)

        def send(cv, clip, row):
            when(sends2, lambda: own2(cv, clip, row).start())
            when(sends1, lambda: own1(cv, clip, row).start())

        def normalize(cv, clip, source, total):
            average, scale = constants(cv, total)

            def step(n, _):
                for i in range(2):
                    row = row_at(n, i)
                    field[cv, clip, 2, row + 1] = normed(cv, source[clip, row], average, scale)
                    if cv == 1:
                        send(cv, clip, row)
                return 0

            lax.fori_loop(0, half, step, 0)
            start_edges(cv, clip, 2)

        def land(cv, clip, n):
            @pl.when(has2)
            def _():
                for i in range(2):
                    row = row_at(n, i)
                    own2(cv, clip, row).wait_recv()
                    when(relays, lambda: relay(cv, clip, row).start())

        def settle(cv, clip, n):
            def take(slot):
                for i in range(2):
                    row = row_at(n, i)
                    if slot == 1:
                        own1(cv, clip, row).wait_recv()
                    if cv == 0:
                        field[cv, clip, slot, row + 1] = normed(
                            cv, raw[clip, slot, row], settled[slot, 0], settled[slot, 1]
                        )

            for slot in range(2):
                when(present[slot], lambda: take(slot))

        def learn(clip):
            def take(slot):
                whole_in_copy = (whole2, whole1)[slot](clip)
                whole_in_copy.wait_recv()
                if slot == 0:
                    when(relays, lambda: whole_relay(clip).start())
                settled[slot, 0], settled[slot, 1] = constants(0, arrived[clip, slot])

            for slot in range(2):
                when(present[slot], lambda: take(slot))

        lead = min(2, half)

        def open_edges(cv, clip):
            early = 1 if bands <= 2 else half
            ahead = max(early, lead if cv == 0 else 1)
            for n in range(1, ahead):
                land(cv, clip, n)
            if cv == 0:
                learn(clip)
            for n in range(early):
                settle(cv, clip, n)
            for slot in (0, 1):
                start_edges(cv, clip, slot)
            for slot in (2, 0, 1):
                wait_edges(cv, clip, slot)
            return early, ahead

        def pairs(cv, clip, body, carry):
            early, ahead = open_edges(cv, clip)

            def step(n, carry):
                @pl.when(jnp.logical_and(n < half, n >= ahead))
                def _():
                    land(cv, clip, n)

                @pl.when(jnp.logical_and(n < half, n >= early))
                def _():
                    settle(cv, clip, n)

                return body(place(n - 1), n, carry)

            return lax.fori_loop(1, half + 1, step, carry)

        column = lax.broadcasted_iota(jnp.int32, (width, 1), 0)

        def convolved(cv, clip, p):
            x = jnp.concatenate(
                [field[cv, clip, slots[f], 2 * p + d] for d in range(4) for f in range(3)], axis=1
            )
            dot = lambda a, b: jnp.dot(a, b, preferred_element_type=jnp.float32)
            y0 = dot(x[:, : 9 * C], weights[cv, : 9 * C, : 2 * C])
            y1 = dot(x, weights[cv, :, 2 * C : 4 * C])
            y2 = dot(x[:, 3 * C :], weights[cv, 3 * C :, 4 * C :])
            bias = scales[3 * cv + 2]

            def joined(left, middle, right):
                left = jnp.where(column >= 1, pltpu.roll(left, 1, 0), 0.0)
                right = jnp.where(column < width - 1, pltpu.roll(right, width - 1, 0), 0.0)
                return middle + left + right + bias

            return (
                joined(y0[:, :C], y0[:, C:], y1[:, :C]),
                joined(y1[:, C:], y2[:, :C], y2[:, C:]),
            )

        def conv_one(clip):
            def step(p, n, carry):
                total, square = carry
                for i, y in enumerate(convolved(0, clip, p)):
                    y = y.astype(jnp.bfloat16)
                    hidden[clip, 2 * p + i] = y
                    y = y.astype(jnp.float32)
                    total = total + folded(y)
                    square = square + folded(y * y)
                return total, square

            zero = jnp.zeros((8, C), jnp.float32)
            start_totals(1, clip, *pairs(0, clip, step, (zero, zero)))

        def conv_two(clip):
            def step(p, n, _):
                for i, y in enumerate(convolved(1, clip, p)):
                    y = y + x_ref[clip, 2 * p + i].astype(jnp.float32)
                    spread[i] = y.astype(jnp.bfloat16).astype(jnp.float32)
                    even = spread[i, pl.ds(0, quarter, stride=2), :]
                    uneven = spread[i, pl.ds(1, quarter, stride=2), :]
                    paired[clip, 2 * p + i] = jnp.concatenate(
                        [even.astype(jnp.bfloat16), uneven.astype(jnp.bfloat16)], axis=1
                    )

                @pl.when(jnp.logical_and(upper, n == 1))
                def _():
                    below(clip).start()

                return 0

            pairs(1, clip, step, 0)

        narrow = lax.broadcasted_iota(jnp.int32, (quarter, 1), 0)

        def downsample(clip):
            when(lower, lambda: below(clip).wait_recv())
            x = jnp.concatenate(
                [
                    jnp.concatenate([paired[clip, 2 * i + a] for a in range(3)], axis=1)
                    for i in range(half)
                ],
                axis=0,
            )
            y = jnp.dot(x, down[...], preferred_element_type=jnp.float32)
            for i in range(half):
                rows = y[i * quarter : (i + 1) * quarter]
                right = pltpu.roll(rows[:, C:], quarter - 1, 0)
                rows = rows[:, :C] + jnp.where(narrow < quarter - 1, right, 0.0) + scales[6]
                out_ref[clip, i] = rows.astype(jnp.bfloat16)

        def send_frames(clip, first, last):
            def step(n, _):
                for i in range(2):
                    send(0, clip, row_at(n, i))
                return 0

            lax.fori_loop(first, last, step, 0)

        pl.semaphore_wait(barrier, expected)
        send_frames(0, 0, lead)
        for clip in range(batch):
            def gather(i, carry):
                v = x_ref[clip, i].astype(jnp.float32)
                return carry[0] + folded(v), carry[1] + folded(v * v)

            zero = jnp.zeros((8, C), jnp.float32)
            frames[clip].wait()
            start_totals(0, clip, *lax.fori_loop(0, height, gather, (zero, zero)))
        for clip in range(batch):
            if clip > 0:
                send_frames(clip, 0, lead)
            whole[clip] = summed(0, clip)
            when(sends2, lambda: whole2(clip).start())
            when(sends1, lambda: whole1(clip).start())
            send_frames(clip, lead, half)
        for vector in vectors:
            vector.wait()
        for clip in range(batch):
            normalize(0, clip, x_ref, whole[clip])
        for load in loads[:conv_loads]:
            load.wait()
        for clip in range(batch):
            if clip == 0:
                land(0, 0, 0)
            conv_one(clip)
            land(*((0, clip + 1) if clip + 1 < batch else (1, 0)), 0)
            normalize(1, clip, hidden, summed(1, clip))
        for load in loads[conv_loads:]:
            load.wait()
        for clip in range(batch):
            conv_two(clip)
            if clip + 1 < batch:
                land(1, clip + 1, 0)
            downsample(clip)

        for cv in range(2):
            for clip in range(batch):
                def leave(q, _):
                    when(sends2, lambda: own2(cv, clip, q).wait_send())
                    when(sends1, lambda: own1(cv, clip, q).wait_send())
                    when(relays, lambda: relay(cv, clip, q).wait_send())
                    return 0

                lax.fori_loop(0, height, leave, 0)
                for slot in range(3):
                    when(both(present[slot], upper), lambda: edge(cv, clip, slot, 0).wait_send())
                    when(both(present[slot], lower), lambda: edge(cv, clip, slot, 1).wait_send())
                for off in range(1, bands):
                    totals(cv, clip, off).wait_send()
        for clip in range(batch):
            when(upper, lambda: below(clip).wait_send())
            when(sends2, lambda: whole2(clip).wait_send())
            when(sends1, lambda: whole1(clip).wait_send())
            when(relays, lambda: whole_relay(clip).wait_send())

    vmem = pl.BlockSpec(memory_space=pltpu.VMEM)
    hbm = pl.BlockSpec(memory_space=pltpu.HBM)
    dma = pltpu.SemaphoreType.DMA
    return pl.pallas_call(
        kernel,
        out_shape=jax.ShapeDtypeStruct((batch, half, quarter, C), jnp.bfloat16),
        in_specs=[hbm] * 11,
        out_specs=vmem,
        scratch_shapes=[
            pltpu.VMEM((batch, height, width, C), jnp.bfloat16),
            pltpu.VMEM((7, 1, C), jnp.float32),
            pltpu.VMEM((batch, 2, height, width, C), jnp.bfloat16),
            pltpu.VMEM((batch, 16, C), jnp.float32),
            pltpu.VMEM((batch, 2, 16, C), jnp.float32),
            pltpu.VMEM((2, 2, 1, C), jnp.float32),
            pltpu.VMEM((2, batch, 3, height + 2, width, C), jnp.bfloat16),
            pltpu.VMEM((2, 12 * C, 6 * C), jnp.bfloat16),
            pltpu.VMEM((6 * C, 2 * C), jnp.bfloat16),
            pltpu.VMEM((batch, height, width, C), jnp.bfloat16),
            pltpu.VMEM((batch, height + 1, quarter, 2 * C), jnp.bfloat16),
            pltpu.VMEM((2, width, C), jnp.float32),
            pltpu.VMEM((2, batch, 16, C), jnp.float32),
            pltpu.VMEM((2, batch, max(bands - 1, 1), 16, C), jnp.float32),
            dma((batch,)),
            dma((7,)),
            dma((45,)),
            dma((2, batch, height)),
            dma((2, batch, height)),
            dma((2, batch, height)),
            dma((2, batch, height)),
            dma((2, batch, height)),
            dma((batch,)),
            dma((batch,)),
            dma((batch,)),
            dma((batch, 2)),
            dma((2, batch, 3, 2)),
            dma((2, batch, 3, 2)),
            dma((2, batch, max(bands - 1, 1))),
            dma((2, batch, max(bands - 1, 1))),
            dma((batch,)),
            dma((batch,)),
        ],
        compiler_params=pltpu.CompilerParams(
            collective_id=0, has_side_effects=True, vmem_limit_bytes=60 * 1024 * 1024
        ),
    )


def solution(mesh):
    steps, bands = mesh.shape["tm"], mesh.shape["rows"]

    def local(
        frames_in,
        gain_one,
        norm_bias_one,
        kernel_one,
        bias_one,
        gain_two,
        norm_bias_two,
        kernel_two,
        bias_two,
        kernel_down,
        bias_down,
    ):
        inputs = frames_in[:, 0]
        batch, height, width, channels = inputs.shape
        vectors = [
            v.reshape(1, channels)
            for v in (
                gain_one, norm_bias_one, bias_one, gain_two, norm_bias_two, bias_two, bias_down
            )
        ]
        wide = (3, 3, 3 * channels, channels)
        call = build(batch, height, width, channels, steps, bands)
        result = call(
            inputs, *vectors, kernel_one.reshape(wide), kernel_two.reshape(wide), kernel_down
        )
        return result[:, None]

    placed = (P("groups", "tm", "rows", None, None),) + (P(),) * 10
    return jax.shard_map(
        local,
        mesh=mesh,
        in_specs=placed,
        out_specs=P("groups", "tm", "rows", None, None),
        check_vma=False,
    )
```

```python
import jax
import jax.numpy as jnp
from jax import lax
from jax.experimental import pallas as pl
from jax.experimental.pallas import tpu as pltpu
from jax.sharding import PartitionSpec as P

G = 32


EPSILON = 1e-06

MESH = pl.DeviceIdType.MESH


def build(batch, height, width, channels, steps, bands):
    half = height // 2
    quarter = width // 2
    C = channels

    def kernel(
        frames_ref, g1_ref, n1_ref, c1_ref, g2_ref, n2_ref, c2_ref, cd_ref,
        k1_ref, k2_ref, kd_ref, out_ref,
        x_ref, scales, raw, whole, arrived, settled, field, weights, down, hidden, paired, spread, sums, others,
        x_sem, scale_sem, k_sem, own2_sem, own1_sem, relay_sem, in2_sem, in1_sem,
        whole2_sem, whole1_sem, whole_relay_sem, whole_in, edge_out, edge_in, sums_out, sums_in, res_out, res_in,
    ):
        t = lax.axis_index("tm")
        r = lax.axis_index("rows")
        has1 = t >= 1
        has2 = t >= 2
        odd = lax.rem(t, 2) == 1
        sends2 = t + 2 < steps
        sends1 = jnp.logical_and(
            t + 1 < steps, jnp.logical_or(jnp.logical_not(odd), t + 2 >= steps)
        )
        relays = jnp.logical_and(odd, has2)
        inner = r > 0

        def place(i):
            return jnp.where(inner, i, half - 1 - i)

        def row_at(n, i):
            return jnp.where(inner, 2 * n + i, height - 1 - 2 * n - i)

        slots = [jnp.maximum(f, 2 - t) for f in range(3)]
        present = [has2, has1, None]

        barrier = pltpu.get_barrier_semaphore()
        expected = bands - 1
        for off in range(1, bands):
            pl.semaphore_signal(
                barrier, inc=1, device_id={"rows": lax.rem(r + off, bands)}, device_id_type=MESH
            )
        for by in (-2, -1, 1, 2):
            there = jnp.logical_and(t + by >= 0, t + by < steps)
            expected = expected + there.astype(jnp.int32)

            @pl.when(there)
            def _():
                pl.semaphore_signal(
                    barrier, inc=1, device_id={"tm": t + by}, device_id_type=MESH
                )

        frames = [
            pltpu.make_async_copy(frames_ref.at[clip], x_ref.at[clip], x_sem.at[clip])
            for clip in range(batch)
        ]
        vectors = [
            pltpu.make_async_copy(ref, scales.at[n], scale_sem.at[n])
            for n, ref in enumerate((g1_ref, n1_ref, c1_ref, g2_ref, n2_ref, c2_ref, cd_ref))
        ]
        for copy in frames + vectors:
            copy.start()

        loads = []
        for cv, k_ref in enumerate((k1_ref, k2_ref)):
            for a in range(3):
                for b in range(3):
                    for o in range(2):
                        loads.append(
                            (
                                k_ref.at[a, b],
                                weights.at[
                                    cv,
                                    pl.ds((a + o) * 3 * C, 3 * C),
                                    pl.ds((o * 3 + b) * C, C),
                                ],
                            )
                        )
        conv_loads = len(loads) // 2
        for a in range(3):
            for b in range(3):
                loads.append(
                    (
                        kd_ref.at[a, b],
                        down.at[
                            pl.ds(a * 2 * C + (C if b == 1 else 0), C),
                            pl.ds(C if b == 2 else 0, C),
                        ],
                    )
                )
        loads = [
            pltpu.make_async_copy(src, dst, k_sem.at[n])
            for n, (src, dst) in enumerate(loads)
        ]
        for load in loads:
            load.start()

        zero_block = jnp.zeros((3 * C, C), jnp.bfloat16)
        for cv in range(2):
            for b in range(3):
                weights[cv, 9 * C : 12 * C, b * C : (b + 1) * C] = zero_block
                weights[cv, 0 : 3 * C, (3 + b) * C : (4 + b) * C] = zero_block
        for a in range(3):
            down[(2 * a + 1) * C : (2 * a + 2) * C, C : 2 * C] = jnp.zeros((C, C), jnp.bfloat16)

        @pl.when(r == 0)
        def _():
            for cv in range(2):
                for clip in range(batch):
                    for f in range(3):
                        field[cv, clip, f, 0] = jnp.zeros((width, C), jnp.bfloat16)

        @pl.when(r == bands - 1)
        def _():
            for cv in range(2):
                for clip in range(batch):
                    for f in range(3):
                        field[cv, clip, f, height + 1] = jnp.zeros((width, C), jnp.bfloat16)
            for clip in range(batch):
                paired[clip, height] = jnp.zeros((quarter, 2 * C), jnp.bfloat16)

        def size_of(cv, clip):
            return 1 if (cv, clip) == (1, batch - 1) else 2

        def starts(cv, clip, n):
            if size_of(cv, clip) == 2:
                return [2 * place(n)]
            return [row_at(n, i) for i in range(2)]

        def landing(cv, clip, slot, row):
            if cv == 0:
                return raw.at[clip, slot, pl.ds(row, size_of(cv, clip))]
            return field.at[cv, clip, slot, pl.ds(row + 1, size_of(cv, clip))]

        def leaving(cv, clip, row):
            if cv == 0:
                return frames_ref.at[clip, pl.ds(row, size_of(cv, clip))]
            return field.at[cv, clip, 2, pl.ds(row + 1, size_of(cv, clip))]

        def own2(cv, clip, q):
            return pltpu.make_async_remote_copy(
                src_ref=leaving(cv, clip, q), dst_ref=landing(cv, clip, 0, q),
                send_sem=own2_sem.at[cv, clip, q], recv_sem=in2_sem.at[cv, clip, q],
                device_id={"tm": t + 2}, device_id_type=MESH,
            )

        def own1(cv, clip, q):
            return pltpu.make_async_remote_copy(
                src_ref=leaving(cv, clip, q), dst_ref=landing(cv, clip, 1, q),
                send_sem=own1_sem.at[cv, clip, q], recv_sem=in1_sem.at[cv, clip, q],
                device_id={"tm": t + 1}, device_id_type=MESH,
            )

        def relay(cv, clip, q):
            return pltpu.make_async_remote_copy(
                src_ref=landing(cv, clip, 0, q), dst_ref=landing(cv, clip, 1, q),
                send_sem=relay_sem.at[cv, clip, q], recv_sem=in1_sem.at[cv, clip, q],
                device_id={"tm": t - 1}, device_id_type=MESH,
            )

        def whole2(clip):
            return pltpu.make_async_remote_copy(
                src_ref=whole.at[clip], dst_ref=arrived.at[clip, 0],
                send_sem=whole2_sem.at[clip], recv_sem=whole_in.at[clip, 0],
                device_id={"tm": t + 2}, device_id_type=MESH,
            )

        def whole1(clip):
            return pltpu.make_async_remote_copy(
                src_ref=whole.at[clip], dst_ref=arrived.at[clip, 1],
                send_sem=whole1_sem.at[clip], recv_sem=whole_in.at[clip, 1],
                device_id={"tm": t + 1}, device_id_type=MESH,
            )

        def whole_relay(clip):
            return pltpu.make_async_remote_copy(
                src_ref=arrived.at[clip, 0], dst_ref=arrived.at[clip, 1],
                send_sem=whole_relay_sem.at[clip], recv_sem=whole_in.at[clip, 1],
                device_id={"tm": t - 1}, device_id_type=MESH,
            )

        def edge(cv, clip, slot, way):
            src, dst, by = ((1, height + 1, -1), (height, 0, 1))[way]
            return pltpu.make_async_remote_copy(
                src_ref=field.at[cv, clip, slot, src], dst_ref=field.at[cv, clip, slot, dst],
                send_sem=edge_out.at[cv, clip, slot, way],
                recv_sem=edge_in.at[cv, clip, slot, way],
                device_id={"rows": r + by}, device_id_type=MESH,
            )

        def totals(cv, clip, off):
            return pltpu.make_async_remote_copy(
                src_ref=sums.at[cv, clip], dst_ref=others.at[cv, clip, off - 1],
                send_sem=sums_out.at[cv, clip, off - 1], recv_sem=sums_in.at[cv, clip, off - 1],
                device_id={"rows": lax.rem(r + off, bands)}, device_id_type=MESH,
            )

        def below(clip):
            return pltpu.make_async_remote_copy(
                src_ref=paired.at[clip, 0], dst_ref=paired.at[clip, height],
                send_sem=res_out.at[clip], recv_sem=res_in.at[clip],
                device_id={"rows": r - 1}, device_id_type=MESH,
            )

        def when(condition, action):
            if condition is None:
                action()
            else:
                pl.when(condition)(action)

        def both(first, second):
            return second if first is None else jnp.logical_and(first, second)

        upper = r > 0
        lower = r < bands - 1

        def start_edges(cv, clip, slot):
            when(both(present[slot], upper), lambda: edge(cv, clip, slot, 0).start())
            when(both(present[slot], lower), lambda: edge(cv, clip, slot, 1).start())

        def wait_edges(cv, clip, slot):
            when(both(present[slot], lower), lambda: edge(cv, clip, slot, 0).wait_recv())
            when(both(present[slot], upper), lambda: edge(cv, clip, slot, 1).wait_recv())

        def folded(values):
            return jnp.sum(values.reshape(width // 8, 8, C), axis=0)

        def start_totals(cv, clip, total, square):
            sums[cv, clip, 0:8] = total
            sums[cv, clip, 8:16] = square
            for off in range(1, bands):
                totals(cv, clip, off).start()

        lane = lax.broadcasted_iota(jnp.int32, (1, C), 1)
        size = C // G

        def grouped(values):
            result = values
            for k in range(1, size):
                left = pltpu.roll(values, k, 1)
                right = pltpu.roll(values, C - k, 1)
                result = result + jnp.where(lax.rem(lane, size) >= k, left, 0.0)
                result = result + jnp.where(lax.rem(lane, size) < size - k, right, 0.0)
            return result

        def summed(cv, clip):
            total = sums[cv, clip]
            for off in range(1, bands):
                totals(cv, clip, off).wait_recv()
                total = total + others[cv, clip, off - 1]
            return total

        def constants(cv, total):
            entries = height * bands * width * size
            sum1 = jnp.broadcast_to(jnp.sum(total[0:8], axis=0, keepdims=True), (8, C))
            sum2 = jnp.broadcast_to(jnp.sum(total[8:16], axis=0, keepdims=True), (8, C))
            average = grouped(sum1)[0:1] / entries
            mean_square = grouped(sum2)[0:1] / entries
            inverse = lax.rsqrt(mean_square - average * average + EPSILON)
            return average, inverse * scales[3 * cv]

        def normed(cv, values, average, scale):
            s = 0.5 * ((values.astype(jnp.float32) - average) * scale + scales[3 * cv + 1])
            return (s + s * jnp.tanh(s)).astype(jnp.bfloat16)

        def send(cv, clip, row):
            when(sends2, lambda: own2(cv, clip, row).start())
            when(sends1, lambda: own1(cv, clip, row).start())

        def normalize(cv, clip, source, total):
            average, scale = constants(cv, total)

            def step(n, _):
                for i in range(2):
                    row = row_at(n, i)
                    field[cv, clip, 2, row + 1] = normed(cv, source[clip, row], average, scale)
                if cv == 1:
                    for row in starts(cv, clip, n):
                        send(cv, clip, row)
                return 0

            lax.fori_loop(0, half, step, 0)
            start_edges(cv, clip, 2)

        def land(cv, clip, n):
            @pl.when(has2)
            def _():
                for row in starts(cv, clip, n):
                    own2(cv, clip, row).wait_recv()
                    when(relays, lambda: relay(cv, clip, row).start())

        def settle(cv, clip, n):
            def take(slot):
                if slot == 1:
                    for row in starts(cv, clip, n):
                        own1(cv, clip, row).wait_recv()
                for i in range(2):
                    row = row_at(n, i)
                    if cv == 0:
                        field[cv, clip, slot, row + 1] = normed(
                            cv, raw[clip, slot, row], settled[slot, 0], settled[slot, 1]
                        )

            for slot in range(2):
                when(present[slot], lambda: take(slot))

        def learn(clip):
            def take(slot):
                whole_in_copy = (whole2, whole1)[slot](clip)
                whole_in_copy.wait_recv()
                if slot == 0:
                    when(relays, lambda: whole_relay(clip).start())
                settled[slot, 0], settled[slot, 1] = constants(0, arrived[clip, slot])

            for slot in range(2):
                when(present[slot], lambda: take(slot))

        lead = min(2, half)

        def open_edges(cv, clip):
            early = 1 if bands <= 2 else half
            ahead = max(early, lead if cv == 0 else 1)
            for n in range(1, ahead):
                land(cv, clip, n)
            if cv == 0:
                learn(clip)
            for n in range(early):
                settle(cv, clip, n)
            for slot in (0, 1):
                start_edges(cv, clip, slot)
            for slot in (2, 0, 1):
                wait_edges(cv, clip, slot)
            return early, ahead

        def pairs(cv, clip, body, carry):
            early, ahead = open_edges(cv, clip)

            def step(n, carry):
                @pl.when(jnp.logical_and(n < half, n >= ahead))
                def _():
                    land(cv, clip, n)

                @pl.when(jnp.logical_and(n < half, n >= early))
                def _():
                    settle(cv, clip, n)

                return body(place(n - 1), n, carry)

            return lax.fori_loop(1, half + 1, step, carry)

        column = lax.broadcasted_iota(jnp.int32, (width, 1), 0)

        def convolved(cv, clip, p):
            x = jnp.concatenate(
                [field[cv, clip, slots[f], 2 * p + d] for d in range(4) for f in range(3)], axis=1
            )
            dot = lambda a, b: jnp.dot(a, b, preferred_element_type=jnp.float32)
            y0 = dot(x[:, : 9 * C], weights[cv, : 9 * C, : 2 * C])
            y1 = dot(x, weights[cv, :, 2 * C : 4 * C])
            y2 = dot(x[:, 3 * C :], weights[cv, 3 * C :, 4 * C :])
            bias = scales[3 * cv + 2]

            def joined(left, middle, right):
                left = jnp.where(column >= 1, pltpu.roll(left, 1, 0), 0.0)
                right = jnp.where(column < width - 1, pltpu.roll(right, width - 1, 0), 0.0)
                return middle + left + right + bias

            return (
                joined(y0[:, :C], y0[:, C:], y1[:, :C]),
                joined(y1[:, C:], y2[:, :C], y2[:, C:]),
            )

        def conv_one(clip):
            def step(p, n, carry):
                total, square = carry
                for i, y in enumerate(convolved(0, clip, p)):
                    y = y.astype(jnp.bfloat16)
                    hidden[clip, 2 * p + i] = y
                    y = y.astype(jnp.float32)
                    total = total + folded(y)
                    square = square + folded(y * y)
                return total, square

            zero = jnp.zeros((8, C), jnp.float32)
            start_totals(1, clip, *pairs(0, clip, step, (zero, zero)))

        def conv_two(clip):
            def step(p, n, _):
                for i, y in enumerate(convolved(1, clip, p)):
                    y = y + x_ref[clip, 2 * p + i].astype(jnp.float32)
                    spread[i] = y.astype(jnp.bfloat16).astype(jnp.float32)
                    even = spread[i, pl.ds(0, quarter, stride=2), :]
                    uneven = spread[i, pl.ds(1, quarter, stride=2), :]
                    paired[clip, 2 * p + i] = jnp.concatenate(
                        [even.astype(jnp.bfloat16), uneven.astype(jnp.bfloat16)], axis=1
                    )

                @pl.when(jnp.logical_and(upper, n == 1))
                def _():
                    below(clip).start()

                return 0

            pairs(1, clip, step, 0)

        narrow = lax.broadcasted_iota(jnp.int32, (quarter, 1), 0)

        def downsample(clip):
            when(lower, lambda: below(clip).wait_recv())
            x = jnp.concatenate(
                [
                    jnp.concatenate([paired[clip, 2 * i + a] for a in range(3)], axis=1)
                    for i in range(half)
                ],
                axis=0,
            )
            y = jnp.dot(x, down[...], preferred_element_type=jnp.float32)
            for i in range(half):
                rows = y[i * quarter : (i + 1) * quarter]
                right = pltpu.roll(rows[:, C:], quarter - 1, 0)
                rows = rows[:, :C] + jnp.where(narrow < quarter - 1, right, 0.0) + scales[6]
                out_ref[clip, i] = rows.astype(jnp.bfloat16)

        def send_frames(clip, first, last):
            def step(n, _):
                for row in starts(0, clip, n):
                    send(0, clip, row)
                return 0

            lax.fori_loop(first, last, step, 0)

        pl.semaphore_wait(barrier, expected)
        send_frames(0, 0, lead)
        for clip in range(batch):
            def gather(i, carry):
                v = x_ref[clip, i].astype(jnp.float32)
                return carry[0] + folded(v), carry[1] + folded(v * v)

            zero = jnp.zeros((8, C), jnp.float32)
            frames[clip].wait()
            start_totals(0, clip, *lax.fori_loop(0, height, gather, (zero, zero)))
        for clip in range(batch):
            if clip > 0:
                send_frames(clip, 0, lead)
            whole[clip] = summed(0, clip)
            when(sends2, lambda: whole2(clip).start())
            when(sends1, lambda: whole1(clip).start())
            send_frames(clip, lead, half)
        for vector in vectors:
            vector.wait()
        for clip in range(batch):
            normalize(0, clip, x_ref, whole[clip])
        for load in loads[:conv_loads]:
            load.wait()
        for clip in range(batch):
            if clip == 0:
                land(0, 0, 0)
            conv_one(clip)
            land(*((0, clip + 1) if clip + 1 < batch else (1, 0)), 0)
            normalize(1, clip, hidden, summed(1, clip))
        for load in loads[conv_loads:]:
            load.wait()
        for clip in range(batch):
            conv_two(clip)
            if clip + 1 < batch:
                land(1, clip + 1, 0)
            downsample(clip)

        for cv in range(2):
            for clip in range(batch):
                def leave(n, _):
                    q = n * size_of(cv, clip)
                    when(sends2, lambda: own2(cv, clip, q).wait_send())
                    when(sends1, lambda: own1(cv, clip, q).wait_send())
                    when(relays, lambda: relay(cv, clip, q).wait_send())
                    return 0

                lax.fori_loop(0, height // size_of(cv, clip), leave, 0)
                for slot in range(3):
                    when(both(present[slot], upper), lambda: edge(cv, clip, slot, 0).wait_send())
                    when(both(present[slot], lower), lambda: edge(cv, clip, slot, 1).wait_send())
                for off in range(1, bands):
                    totals(cv, clip, off).wait_send()
        for clip in range(batch):
            when(upper, lambda: below(clip).wait_send())
            when(sends2, lambda: whole2(clip).wait_send())
            when(sends1, lambda: whole1(clip).wait_send())
            when(relays, lambda: whole_relay(clip).wait_send())

    vmem = pl.BlockSpec(memory_space=pltpu.VMEM)
    hbm = pl.BlockSpec(memory_space=pltpu.HBM)
    dma = pltpu.SemaphoreType.DMA
    return pl.pallas_call(
        kernel,
        out_shape=jax.ShapeDtypeStruct((batch, half, quarter, C), jnp.bfloat16),
        in_specs=[hbm] * 11,
        out_specs=vmem,
        scratch_shapes=[
            pltpu.VMEM((batch, height, width, C), jnp.bfloat16),
            pltpu.VMEM((7, 1, C), jnp.float32),
            pltpu.VMEM((batch, 2, height, width, C), jnp.bfloat16),
            pltpu.VMEM((batch, 16, C), jnp.float32),
            pltpu.VMEM((batch, 2, 16, C), jnp.float32),
            pltpu.VMEM((2, 2, 1, C), jnp.float32),
            pltpu.VMEM((2, batch, 3, height + 2, width, C), jnp.bfloat16),
            pltpu.VMEM((2, 12 * C, 6 * C), jnp.bfloat16),
            pltpu.VMEM((6 * C, 2 * C), jnp.bfloat16),
            pltpu.VMEM((batch, height, width, C), jnp.bfloat16),
            pltpu.VMEM((batch, height + 1, quarter, 2 * C), jnp.bfloat16),
            pltpu.VMEM((2, width, C), jnp.float32),
            pltpu.VMEM((2, batch, 16, C), jnp.float32),
            pltpu.VMEM((2, batch, max(bands - 1, 1), 16, C), jnp.float32),
            dma((batch,)),
            dma((7,)),
            dma((45,)),
            dma((2, batch, height)),
            dma((2, batch, height)),
            dma((2, batch, height)),
            dma((2, batch, height)),
            dma((2, batch, height)),
            dma((batch,)),
            dma((batch,)),
            dma((batch,)),
            dma((batch, 2)),
            dma((2, batch, 3, 2)),
            dma((2, batch, 3, 2)),
            dma((2, batch, max(bands - 1, 1))),
            dma((2, batch, max(bands - 1, 1))),
            dma((batch,)),
            dma((batch,)),
        ],
        compiler_params=pltpu.CompilerParams(
            collective_id=0, has_side_effects=True, vmem_limit_bytes=60 * 1024 * 1024
        ),
    )


def solution(mesh):
    steps, bands = mesh.shape["tm"], mesh.shape["rows"]

    def local(
        frames_in,
        gain_one,
        norm_bias_one,
        kernel_one,
        bias_one,
        gain_two,
        norm_bias_two,
        kernel_two,
        bias_two,
        kernel_down,
        bias_down,
    ):
        inputs = frames_in[:, 0]
        batch, height, width, channels = inputs.shape
        vectors = [
            v.reshape(1, channels)
            for v in (
                gain_one, norm_bias_one, bias_one, gain_two, norm_bias_two, bias_two, bias_down
            )
        ]
        wide = (3, 3, 3 * channels, channels)
        call = build(batch, height, width, channels, steps, bands)
        result = call(
            inputs, *vectors, kernel_one.reshape(wide), kernel_two.reshape(wide), kernel_down
        )
        return result[:, None]

    placed = (P("groups", "tm", "rows", None, None),) + (P(),) * 10
    return jax.shard_map(
        local,
        mesh=mesh,
        in_specs=placed,
        out_specs=P("groups", "tm", "rows", None, None),
        check_vma=False,
    )
```
